32 devices in a mesh: ep: 16 (over z, x, core), tp: 2 (over y).
Axes of the slice: x: 2, y: 2, z: 4, core: 2. Of those that a mesh axis runs over, the one named last changes fastest.
Arguments:
- hidden_in: bfloat16 [2048, 2048], P('ep', 'tp'), may hold values from -50 to 50
- norm_gain: float32 [2048], P('tp'), may hold values from 0.5 to 1.5
- expert_ids: int32 [2048, 8], P('ep'), may hold values from 0 to 31, all different within a row; in each aligned block of 128 rows (0 to 127, 128 to 255, ...) at most 48 rows name the same one
- routing_weight: float32 [2048, 8], P('ep'), may hold values from 0.03 to 0.3
- labels: int32 [2048], P('ep'), may hold values from 0 to 3
- grad_later: bfloat16 [2048, 2048], P('ep', 'tp'), may hold values from -6 to 6
- head_weight: bfloat16 [2048, 4], P('tp'), may hold values from -0.125 to 0.125
- gate_weight: bfloat16 [24576, 2048], P(('ep', 'tp')), may hold values from -0.125 to 0.125
- up_weight: bfloat16 [24576, 2048], P(('ep', 'tp')), may hold values from -0.125 to 0.125
- down_weight: bfloat16 [24576, 2048], P(('ep', 'tp')), may hold values from -0.21875 to 0.21875
Outputs:
- token_loss: float32 [2048], P('ep')
- outcome: bfloat16 [2048, 2048], P('ep', 'tp')
- grad_input: bfloat16 [2048, 2048], P('ep', 'tp')
- grad_gate: bfloat16 [24576, 2048], P(('ep', 'tp'))
- grad_up: bfloat16 [24576, 2048], P(('ep', 'tp'))
- grad_down: bfloat16 [24576, 2048], P(('ep', 'tp'))
The draws below stay inside these ranges and needn't reach their ends.
Inputs may be any that keep to these rules, and one draw needn't show every extreme that they name: `expert_ids`: each row names 8 different experts. Within the 128 rows of one index of ep, no expert is named more than 48 times, a bound that some block reaches.
All inputs are finite; a program needn't handle non-finite values.
Results may differ from the reference program's by a relative error of at most 0.011.
Values may be sent and summed in bfloat16 or wider, within the bound.
No kernel may reach another device: no remote copies, remote signals or barrier semaphores. Data moves between devices by JAX's collectives and lax.ppermute only.
A program may use at most 128 MiB of HBM per device.

```python
import math
import jax
import jax.numpy as jnp
import numpy as np
from jax import lax

D = 2048
FF = 768
TOP = 8
LABELS = 4
TOK_DEV = 128
EXPERTS = 32
UNITS = 768
CAP = 48
TOKENS = 2048
N_EP = 16


def draw_hidden_in(key, part):
    key_base, key_row, key_col = jax.random.split(key, 3)
    position = jnp.arange(D, dtype=jnp.float32) / D
    base = jnp.clip(jax.random.normal(key_base, (TOKENS, D), jnp.float32), -5.0, 5.0)
    row_scale = jnp.exp(jax.random.uniform(key_row, (TOKENS, 1), jnp.float32, 0.0, math.log(10.0))) / 3.0
    col_scale = jnp.exp(jax.random.uniform(key_col, (1, D), jnp.float32, 0.0, math.log(10.0))) * (3.0 ** position)[None, :]
    return (base * row_scale * col_scale / 12.0).astype(jnp.bfloat16)


def plant(drawn, rng, low, largest):
    extent = drawn.shape
    index_at = [jax.random.randint(jax.random.fold_in(rng, axis), (), 0, extent[axis]) for axis in range(len(extent))]
    drawn = drawn.at[tuple(index_at)].set(low)
    longest = extent.index(max(extent))
    index_at[longest] = (index_at[longest] + 1) % extent[longest]
    return drawn.at[tuple(index_at)].set(largest)


def block_scale(own_key, dims, cuts, smallest, high):
    level, own = 1.0, jax.random.fold_in(own_key, 6)
    for dim, blocks in cuts:
        heights = jnp.exp(jax.random.uniform(jax.random.fold_in(own, dim), (blocks,), jnp.float32, smallest / len(cuts), high / len(cuts)))
        level = level * jnp.repeat(heights, dims[dim] // blocks).reshape([-1 if axis == dim else 1 for axis in range(len(dims))])
    return level


def assign_block(rng, own, number, rows, number_of, top, reach, skew):
    order = jax.random.permutation(rng, number_of)
    crowded, usual = load_shares(number_of, rows * top, reach, skew, True), load_shares(number_of, rows * top, reach, skew, False)
    places = jnp.arange(number_of)

    def named(sizes, turn):
        used = int((sizes > 0).sum())
        fixed = max(1, used // 4)
        shifted = fixed + (places - fixed + turn * (used - fixed)) % max(1, number_of - fixed)
        return jnp.zeros((number_of,), jnp.int32).at[order[jnp.where(places < fixed, places, shifted)]].set(jnp.asarray(sizes, jnp.int32))

    sizes = jnp.where(number % 4 == 0, named(crowded, number // 4), named(usual, number - number // 4 - 1))
    mixed = jax.random.permutation(jax.random.fold_in(own, 3), number_of)
    giver, receiver = mixed[0:number_of // 2 * 2:2], mixed[1:number_of // 2 * 2:2]
    room = jnp.minimum(sizes[giver] - 1, reach - sizes[receiver]) // 2
    room = jnp.where((giver == order[0]) | (receiver == order[0]) | (sizes[receiver] == 0), 0, jnp.maximum(room, 0))
    shifted = jax.random.randint(jax.random.fold_in(own, 4), (number_of // 2,), 0, 1 << 20) % (room + 1)
    sizes = sizes.at[giver].add(-shifted).at[receiver].add(shifted)
    items = jnp.searchsorted(jnp.cumsum(sizes), jnp.arange(rows * top), side="right").astype(jnp.int32)
    grid = items.reshape(top, rows).T
    grid = grid[jax.random.permutation(jax.random.fold_in(own, 1), rows)]
    turn = jax.random.randint(jax.random.fold_in(own, 2), (rows, 1), 0, top)
    return jnp.take_along_axis(grid, (jnp.arange(top)[None, :] + turn) % top, axis=1)


def load_shares(count, total, limit, skew, full):
    loads = [(1 << 20) // math.isqrt(rank ** skew) + 1 for rank in range(1, count + 1)]
    largest = limit if full else min(limit, max(-(-total // count), total * loads[0] // sum(loads)))
    least = 1 if total - largest >= count - 1 else 0
    holding, rest = [largest] + [least] * (count - 1), total - largest - least * (count - 1)
    while rest > 0:
        candidates = [i for i in range(1, count) if holding[i] < largest] or [i for i in range(1, count) if holding[i] < limit]
        mass, left = sum([loads[i] for i in candidates]), rest
        for i in candidates:
            addition = min(limit - holding[i], max(1, left * loads[i] // mass), rest)
            holding[i] = holding[i] + addition
            rest = rest - addition
    return np.array(holding)


def normal_values(stream_key, extent, deviation, bound, cuts=(), kind=jnp.bfloat16):
    entries = jax.random.normal(stream_key, extent, jnp.float32) * deviation
    if len(cuts) > 0:
        entries = block_scale(stream_key, extent, cuts, -0.22, 0.18) * entries
    return jnp.clip(entries, min=-bound, max=bound).astype(kind)


def setup_inputs(seed: int = 0) -> dict:
    splits = jax.random.split(jax.random.key(seed), 11)
    hidden_in = draw_hidden_in(jax.random.fold_in(splits[10], 71), 0)
    norm_gain = jnp.clip(1.0 + 0.1 * jax.random.normal(splits[1], (D,), jnp.float32), 0.5, 1.5)
    expert_ids_keys = jax.random.split(jax.random.fold_in(splits[2], 1), TOKENS // TOK_DEV)
    expert_ids_turns = jax.random.permutation(jax.random.fold_in(splits[2], 3), TOKENS // TOK_DEV)
    expert_ids = jax.vmap(lambda own, number: assign_block(jax.random.fold_in(splits[2], 2), own, number, TOK_DEV, EXPERTS, TOP, CAP, 2))(expert_ids_keys, expert_ids_turns).reshape((TOKENS, TOP))
    routing_weight = jnp.clip(jnp.exp(math.log(0.3) - 2.3025852 * jax.random.uniform(splits[3], (TOKENS, TOP), jnp.float32) ** block_scale(splits[3], (TOKENS, TOP), ((0, 16),), -0.2, 0.2)), 0.03, 0.3)
    labels = plant(jax.random.randint(splits[4], (TOKENS,), 0, LABELS), jax.random.fold_in(splits[4], 1), 0, LABELS - 1).astype(jnp.int32)
    grad_later = normal_values(splits[5], (TOKENS, D), 1.0, 6.0, ((0, 16), (1, 2)))
    head_weight = normal_values(splits[6], (D, LABELS), D ** -0.5, 0.125, ((0, 2),))
    gate_weight = normal_values(splits[7], (EXPERTS * FF, D), D ** -0.5, 0.125, ((0, 32),))
    up_weight = normal_values(splits[8], (EXPERTS * FF, D), D ** -0.5, 0.125, ((0, 32),))
    down_weight = normal_values(splits[9], (EXPERTS * FF, D), FF ** -0.5, 0.21875, ((0, 32),))
    return {"hidden_in": hidden_in, "norm_gain": norm_gain, "expert_ids": expert_ids, "routing_weight": routing_weight, "labels": labels, "grad_later": grad_later, "head_weight": head_weight, "gate_weight": gate_weight, "up_weight": up_weight, "down_weight": down_weight}


EPS = 1e-06
LOSS_SCALE = 64.0

def slot_numbers(expert_ids):
    blocks = expert_ids.reshape(N_EP, TOK_DEV * TOP)

    def per_device(block):
        marks = (block[:, None] == jnp.arange(EXPERTS, dtype=jnp.int32)[None, :]).astype(jnp.int32)
        before = jnp.cumsum(marks, axis=0) - marks
        return lax.optimization_barrier(jnp.sum(before * marks, axis=1)).astype(jnp.int32)
    return lax.map(per_device, blocks).reshape(TOKENS, TOP)

def expert_forward(packed):
    inputs, w_gate, w_up, w_down = packed
    gate_pre = jnp.dot(inputs, w_gate.T, preferred_element_type=jnp.float32)
    up_pre = jnp.dot(inputs, w_up.T, preferred_element_type=jnp.float32)
    sigma = jax.nn.sigmoid(gate_pre)
    active = (gate_pre * sigma * up_pre).astype(jnp.bfloat16)
    output = jnp.zeros((inputs.shape[0], D), jnp.float32)
    for group in range(FF // UNITS):
        start_col = group * UNITS
        part_sum = jnp.dot(active[:, start_col:start_col + UNITS], w_down[start_col:start_col + UNITS, :], preferred_element_type=jnp.float32).astype(jnp.bfloat16)
        output = output + lax.optimization_barrier(part_sum).astype(jnp.float32)
    return output

def expert_backward(packed):
    inputs, grads_in, w_gate, w_up, w_down = packed
    gate_pre = jnp.dot(inputs, w_gate.T, preferred_element_type=jnp.float32)
    up_pre = jnp.dot(inputs, w_up.T, preferred_element_type=jnp.float32)
    sigma = jax.nn.sigmoid(gate_pre)
    active = (gate_pre * sigma * up_pre).astype(jnp.bfloat16)
    d_active = jnp.dot(grads_in, w_down.T, preferred_element_type=jnp.float32)
    grad_down = jnp.dot(active.T, grads_in, preferred_element_type=jnp.float32).astype(jnp.bfloat16)
    d_gate = (d_active * up_pre * sigma * (1.0 + gate_pre * (1.0 - sigma))).astype(jnp.bfloat16)
    d_up = (d_active * gate_pre * sigma).astype(jnp.bfloat16)
    grad_gate = jnp.dot(d_gate.T, inputs, preferred_element_type=jnp.float32).astype(jnp.bfloat16)
    grad_up = jnp.dot(d_up.T, inputs, preferred_element_type=jnp.float32).astype(jnp.bfloat16)
    d_inputs = jnp.zeros((inputs.shape[0], D), jnp.float32)
    for group in range(FF // UNITS):
        start_col = group * UNITS
        part_sum = (jnp.dot(d_gate[:, start_col:start_col + UNITS], w_gate[start_col:start_col + UNITS, :], preferred_element_type=jnp.float32) + jnp.dot(d_up[:, start_col:start_col + UNITS], w_up[start_col:start_col + UNITS, :], preferred_element_type=jnp.float32)).astype(jnp.bfloat16)
        d_inputs = d_inputs + lax.optimization_barrier(part_sum).astype(jnp.float32)
    return (grad_gate, grad_up, grad_down, d_inputs)

def reference(hidden_in, norm_gain, expert_ids, routing_weight, labels, grad_later, head_weight, gate_weight, up_weight, down_weight):
    gate_three = gate_weight.reshape(EXPERTS, FF, D)
    up_three = up_weight.reshape(EXPERTS, FF, D)
    down_three = down_weight.reshape(EXPERTS, FF, D)
    hidden_wide = hidden_in.astype(jnp.float32)
    inv_rms = lax.rsqrt(lax.optimization_barrier(jnp.sum(hidden_wide * hidden_wide, axis=1, keepdims=True)) / D + EPS)
    normed = (hidden_wide * inv_rms * norm_gain[None, :]).astype(jnp.bfloat16)
    slots = slot_numbers(expert_ids)
    source = (jnp.arange(TOKENS, dtype=jnp.int32) // TOK_DEV).astype(jnp.int32)[:, None]
    rows_each = N_EP * CAP
    targets = (expert_ids * rows_each + source * CAP + slots).astype(jnp.int32)
    buffer = jnp.zeros((EXPERTS * rows_each, D), jnp.bfloat16)
    for slot_rank in range(TOP):
        buffer = buffer.at[targets[:, slot_rank]].set(normed)
    buffer = buffer.reshape(EXPERTS, rows_each, D)
    outputs = lax.map(expert_forward, (buffer, gate_three, up_three, down_three)).reshape(EXPERTS * rows_each, D)
    mixed = jnp.zeros((TOKENS, D), jnp.float32)
    for slot_rank in range(TOP):
        mixed = mixed + routing_weight[:, slot_rank:slot_rank + 1] * outputs[targets[:, slot_rank]]
    outcome = (hidden_wide + mixed).astype(jnp.bfloat16)
    logits = jnp.dot(outcome, head_weight, preferred_element_type=jnp.float32)
    classes = (labels[:, None] == jnp.arange(LABELS, dtype=jnp.int32)[None, :]).astype(jnp.float32)
    totals = lax.optimization_barrier(jnp.sum(jnp.exp(logits), axis=1, keepdims=True))
    token_loss = jnp.log(totals[:, 0]) - lax.optimization_barrier(jnp.sum(logits * classes, axis=1))
    d_logits = (jnp.exp(logits) / totals - classes) * LOSS_SCALE
    d_outcome = jnp.dot(d_logits, head_weight.astype(jnp.float32).T, precision=lax.Precision.HIGHEST) + grad_later.astype(jnp.float32)
    d_rounded = lax.optimization_barrier(d_outcome.astype(jnp.bfloat16)).astype(jnp.float32)
    grad_buffer = jnp.zeros((EXPERTS * rows_each, D), jnp.bfloat16)
    for slot_rank in range(TOP):
        scaled_rows = (routing_weight[:, slot_rank:slot_rank + 1] * d_rounded).astype(jnp.bfloat16)
        grad_buffer = grad_buffer.at[targets[:, slot_rank]].set(scaled_rows)
    grad_buffer = grad_buffer.reshape(EXPERTS, rows_each, D)
    grad_gate, grad_up, grad_down, d_inputs = lax.map(expert_backward, (buffer, grad_buffer, gate_three, up_three, down_three))
    d_inputs = d_inputs.reshape(EXPERTS * rows_each, D)
    d_normed = jnp.zeros((TOKENS, D), jnp.float32)
    for slot_rank in range(TOP):
        d_normed = d_normed + d_inputs[targets[:, slot_rank]]
    d_scaled = d_normed * norm_gain[None, :]
    slope = lax.optimization_barrier(jnp.sum(d_scaled * hidden_wide, axis=1, keepdims=True)) / D
    d_hidden = inv_rms * d_scaled - hidden_wide * (inv_rms * inv_rms * inv_rms) * slope
    grad_input = (d_outcome + d_hidden).astype(jnp.bfloat16)
    return (token_loss, outcome, grad_input, grad_gate.reshape(EXPERTS * FF, D), grad_up.reshape(EXPERTS * FF, D), grad_down.reshape(EXPERTS * FF, D))
```

```python
import jax
import jax.numpy as jnp
from jax import lax
from jax.sharding import PartitionSpec as P

FF = 768

EPS = 1e-06
LOSS_SCALE = 64.0
BF = jnp.bfloat16
F32 = jnp.float32
EXACT = lax.Precision.HIGHEST


def ring_sizes(dev_count):
    chips = dev_count // 2
    across = 1
    while across * across * 4 <= chips:
        across *= 2
    return 2, across, chips // across


def send_ep(value, mask):
    pairs = [(i, i ^ mask) for i in range(lax.axis_size("ep"))]
    return lax.ppermute(value, "ep", pairs)


def send_tp(value, mask):
    pairs = [(i, i ^ mask) for i in range(lax.axis_size("tp"))]
    return lax.ppermute(value, "tp", pairs)


def spread_ep(value, stride, count):
    parts = [value] + [send_ep(value, k * stride) for k in range(1, count)]
    return jnp.stack(parts)


def xor_blocks(value, axis, index):
    size = value.shape[axis]
    bit = 1
    while bit < size:
        shape = value.shape
        split = shape[:axis] + (size // (2 * bit), 2, bit) + shape[axis + 1 :]
        pairs = value.reshape(split)
        turned = jnp.flip(pairs, axis + 1)
        value = jnp.where((index & bit) > 0, turned, pairs).reshape(shape)
        bit *= 2
    return value


class Routes:
    def __init__(self, meta, top_count, capacity, sizes, expert_of):
        self.sizes = sizes
        self.capacity = capacity
        self.ids = meta[..., :top_count, :]
        self.weights = meta[..., top_count : 2 * top_count, :]
        tok_count = meta.shape[-1]
        place = jnp.arange(tok_count, dtype=jnp.int32)
        self.earlier = (place[:, None] < place[None, :]).astype(BF)
        self.expert_of = expert_of

    def picks(self, expert, ids):
        named = (ids == expert.astype(F32)).astype(F32)
        member = jnp.sum(named, axis=-2)
        before = lax.dot_general(
            member.astype(BF),
            self.earlier,
            (((member.ndim - 1,), (0,)), ((), ())),
            preferred_element_type=F32,
        )
        slots = jnp.arange(self.capacity, dtype=F32)[:, None]
        chosen = jnp.logical_and(before[..., None, :] == slots, member[..., None, :] > 0)
        return chosen.astype(F32), named


def gather_rows(value, routes, picks_a, picks_b, col):
    cores, across, depth = routes.sizes
    tp = lax.axis_size("tp")
    cap = routes.capacity
    half = value.shape[1] // 2
    column = spread_ep(value, 2 * across, depth)
    side_a = spread_ep(column[..., :half], 2, across)
    side_b = jnp.stack([column[..., half:]] + [send_tp(column[..., half:], j) for j in range(1, tp)], axis=2)
    full_a = spread_ep(side_a, 1, cores)
    full_b = spread_ep(side_b, 1, cores)
    rows_a = jnp.einsum("cxzst,cxztd->cxzsd", picks_a, full_a, preferred_element_type=BF)
    rows_b = jnp.einsum("czst,cztjd->czsjd", picks_b, full_b, preferred_element_type=BF)
    parts_a = [rows_a[..., :cap, :]] + [
        send_tp(rows_a[..., j * cap : (j + 1) * cap, :], j) for j in range(1, tp)
    ]
    parts_b = [rows_b[:, :, :cap]] + [
        send_ep(rows_b[:, :, k * cap : (k + 1) * cap], 2 * k) for k in range(1, across)
    ]
    whole_a = jnp.stack(parts_a, axis=4)
    whole_b = jnp.stack(parts_b, axis=1)
    whole = jnp.concatenate([whole_a, whole_b], axis=-1)
    return xor_blocks(whole, 4, col)


def return_rows(rows, routes, picks_a, picks_b, col):
    cores, across, depth = routes.sizes
    tp = lax.axis_size("tp")
    half = rows.shape[-1] // 2
    rows = xor_blocks(rows, 4, col)
    part_a, part_b = rows[..., :half], rows[..., half:]
    cat_a = jnp.concatenate(
        [part_a[..., 0, :]] + [send_tp(part_a[..., j, :], j) for j in range(1, tp)], axis=3
    )
    cat_b = jnp.concatenate(
        [part_b[:, 0]] + [send_ep(part_b[:, k], 2 * k) for k in range(1, across)], axis=2
    )
    sum_a = jnp.einsum("cxzst,cxzsd->cxztd", picks_a, cat_a, preferred_element_type=BF)
    sum_b = jnp.einsum("czst,czsjd->cjztd", picks_b, cat_b, preferred_element_type=BF)

    def add_core(value):
        return (value[0].astype(F32) + send_ep(value[1], 1).astype(F32)).astype(BF)

    sum_a = add_core(sum_a)
    sum_b = add_core(sum_b)
    total_a = sum_a[0].astype(F32)
    for k in range(1, across):
        total_a = total_a + send_ep(sum_a[k], 2 * k).astype(F32)
    total_b = sum_b[0].astype(F32)
    for j in range(1, tp):
        total_b = total_b + send_tp(sum_b[j], j).astype(F32)
    column = jnp.concatenate([total_a.astype(BF), total_b.astype(BF)], axis=-1)
    result = column[0].astype(F32)
    for k in range(1, depth):
        result = result + send_ep(column[k], 2 * across * k).astype(F32)
    return result


def sum_all(value):
    step = 1
    while step < lax.axis_size("ep"):
        value = value + send_ep(value, step)
        step *= 2
    step = 1
    while step < lax.axis_size("tp"):
        value = value + send_tp(value, step)
        step *= 2
    return value


def shards(
    hidden_in,
    norm_gain,
    expert_ids,
    routing_weight,
    labels,
    grad_later,
    head_weight,
    gate_weight,
    up_weight,
    down_weight,
):
    dev_count = lax.axis_size("ep")
    tp = lax.axis_size("tp")
    row, col = lax.axis_index("ep"), lax.axis_index("tp")
    sizes = ring_sizes(dev_count)
    cores, across, depth = sizes
    tok_count, width = hidden_in.shape
    top_count = expert_ids.shape[1]
    model_width = gate_weight.shape[1]
    unit_rows = gate_weight.shape[0]
    local_count = unit_rows * tp // FF
    expert_count = local_count * dev_count
    capacity = tok_count * top_count * 3 // (2 * expert_count)
    row_count = dev_count * capacity
    label_count = head_weight.shape[1]

    def expert_of(ep_index, tp_index):
        return ep_index * local_count + tp_index * unit_rows // FF

    spare = -(2 * top_count + 1) % 8
    meta = jnp.concatenate(
        [
            expert_ids.T.astype(F32),
            routing_weight.T,
            labels.astype(F32)[None, :],
            jnp.zeros((spare, tok_count), F32),
        ]
    )
    meta = spread_ep(spread_ep(spread_ep(meta, 2 * across, depth), 2, across), 1, cores)
    feature_rows = jnp.concatenate(
        [
            norm_gain[None, :],
            head_weight.astype(F32).T,
            jnp.zeros((-(1 + label_count) % 8, width), F32),
        ]
    )
    own_gain, own_head = feature_rows[0], feature_rows[1 : 1 + label_count]
    all_features = jnp.stack([feature_rows] + [send_tp(feature_rows, j) for j in range(1, tp)], axis=1)
    all_features = xor_blocks(all_features, 1, col).reshape(feature_rows.shape[0], model_width)
    gain = all_features[0]
    head = all_features[1 : 1 + label_count]

    routes = Routes(meta, top_count, capacity, sizes, expert_of)
    ids_near = routes.ids[:, 0]
    picks_own, named_own = routes.picks(expert_of(row, col), routes.ids)
    picks_a = jnp.concatenate(
        [picks_own] + [routes.picks(expert_of(row, col ^ j), routes.ids)[0] for j in range(1, tp)], axis=3
    ).astype(BF)
    picks_b = jnp.concatenate(
        [picks_own[:, 0]]
        + [routes.picks(expert_of(row ^ (2 * k), col), ids_near)[0] for k in range(1, across)],
        axis=2,
    ).astype(BF)
    scale_own = jnp.sum(named_own * routes.weights, axis=-2)
    scales = jnp.sum(picks_own * scale_own[..., None, :], axis=-1).reshape(row_count, 1)
    label_all = meta[..., 2 * top_count, :]

    hidden_wide = hidden_in.astype(F32)
    squares = jnp.sum(hidden_wide * hidden_wide, axis=1)
    for j in range(1, tp):
        squares = squares + send_tp(jnp.sum(hidden_wide * hidden_wide, axis=1), j)
    inv_rms = lax.rsqrt(squares / model_width + EPS)[:, None]

    rows_in = gather_rows(hidden_in, routes, picks_a, picks_b, col).reshape(row_count, model_width)
    later_rows = gather_rows(grad_later, routes, picks_a, picks_b, col).reshape(row_count, model_width)
    rows_wide = rows_in.astype(F32)
    row_rms = lax.rsqrt(jnp.sum(rows_wide * rows_wide, axis=1, keepdims=True) / model_width + EPS)
    received = (rows_wide * row_rms * gain[None, :]).astype(BF)

    def against(left, right):
        return lax.dot_general(left, right, (((1,), (1,)), ((), ())), preferred_element_type=F32)

    def over_rows(left, right):
        return lax.dot_general(left, right, (((0,), (0,)), ((), ())), preferred_element_type=F32).astype(BF)

    gate_pre = against(received, gate_weight)
    up_pre = against(received, up_weight)
    sigma = jax.nn.sigmoid(gate_pre)
    active = (gate_pre * sigma * up_pre).astype(BF)

    down_head = lax.dot_general(
        head.astype(BF), down_weight, (((1,), (1,)), ((), ())), preferred_element_type=F32
    )
    row_logits = lax.dot_general(
        active.astype(F32), down_head, (((1,), (1,)), ((), ())), precision=EXACT, preferred_element_type=F32
    )
    row_logits = (row_logits * scales).reshape(cores, across, depth, capacity, label_count)
    logits = jnp.einsum("cxzst,cxzsl->cxzlt", picks_own, row_logits, precision=EXACT)
    own_logits = lax.dot_general(
        own_head.astype(BF), hidden_in, (((1,), (1,)), ((), ())), preferred_element_type=F32
    )

    def turn(value):
        value = xor_blocks(value, 0, row & 1)
        value = xor_blocks(value, 1, (row // 2) & (across - 1))
        return xor_blocks(value, 2, row // (2 * across))

    at_own = (
        (jnp.arange(cores)[:, None, None] == 0)
        & (jnp.arange(across)[None, :, None] == 0)
        & (jnp.arange(depth)[None, None, :] == 0)
    )
    logits = logits + jnp.where(at_own[..., None, None], own_logits, 0.0)
    logits = turn(sum_all(turn(logits)))
    classes = (label_all[..., None, :] == jnp.arange(label_count, dtype=F32)[:, None]).astype(F32)
    powers = jnp.exp(logits)
    totals = jnp.sum(powers, axis=-2, keepdims=True)
    d_logits = (powers / totals - classes) * LOSS_SCALE
    token_loss = jnp.log(totals[0, 0, 0, 0]) - jnp.sum(logits[0, 0, 0] * classes[0, 0, 0], axis=0)
    row_d_logits = jnp.einsum("cxzst,cxzlt->cxzsl", picks_own, d_logits, precision=EXACT)
    d_rounded = (
        lax.dot_general(
            row_d_logits.reshape(row_count, label_count), head, (((1,), (0,)), ((), ())), precision=EXACT
        )
        + later_rows.astype(F32)
    ).astype(BF)
    grads_in = (scales * d_rounded.astype(F32)).astype(BF)

    d_active = against(grads_in, down_weight)
    d_gate = (d_active * up_pre * sigma * (1.0 + gate_pre * (1.0 - sigma))).astype(BF)
    d_up = (d_active * gate_pre * sigma).astype(BF)

    def times(left, right):
        return lax.dot_general(left, right, (((1,), (0,)), ((), ())), preferred_element_type=F32)

    def as_rows(value):
        return value.reshape(cores, across, depth, capacity, tp, width)

    d_rows = (times(d_gate, gate_weight) + times(d_up, up_weight)).astype(BF)
    d_normed = return_rows(as_rows(d_rows), routes, picks_a, picks_b, col)
    out_rows = (times(active, down_weight) * scales).astype(BF)
    mixed = return_rows(as_rows(out_rows), routes, picks_a, picks_b, col)

    grad_down = over_rows(active, grads_in)
    grad_gate = over_rows(d_gate, received)
    grad_up = over_rows(d_up, received)

    outcome = (hidden_wide + mixed).astype(BF)
    d_outcome = lax.dot_general(
        d_logits[0, 0, 0], own_head, (((0,), (0,)), ((), ())), precision=EXACT
    ) + grad_later.astype(F32)
    d_scaled = d_normed * own_gain[None, :]
    products = jnp.sum(d_scaled * hidden_wide, axis=1)
    slope = products
    for j in range(1, tp):
        slope = slope + send_tp(products, j)
    slope = slope[:, None] / model_width
    d_hidden = inv_rms * d_scaled - hidden_wide * (inv_rms * inv_rms * inv_rms) * slope
    grad_input = (d_outcome + d_hidden).astype(BF)
    return token_loss, outcome, grad_input, grad_gate, grad_up, grad_down


def solution(mesh):
    in_specs = (
        P("ep", "tp"),
        P("tp"),
        P("ep", None),
        P("ep", None),
        P("ep"),
        P("ep", "tp"),
        P("tp", None),
        P(("ep", "tp"), None),
        P(("ep", "tp"), None),
        P(("ep", "tp"), None),
    )
    out_specs = (
        P("ep"),
        P("ep", "tp"),
        P("ep", "tp"),
        P(("ep", "tp"), None),
        P(("ep", "tp"), None),
        P(("ep", "tp"), None),
    )
    return jax.shard_map(shards, mesh=mesh, in_specs=in_specs, out_specs=out_specs, check_vma=False)
```

```python
import functools

import jax
import jax.numpy as jnp
from jax import lax
from jax.experimental import pallas as pl
from jax.experimental.pallas import tpu as pltpu
from jax.sharding import PartitionSpec as P

FF = 768

EPS = 1e-06
LOSS_SCALE = 64.0
BF = jnp.bfloat16
F32 = jnp.float32
EXACT = lax.Precision.HIGHEST
VMEM_BYTES = 24 * 1024 * 1024
LANES = 128


def ring_sizes(dev_count):
    chips = dev_count // 2
    across = 1
    while across * across * 4 <= chips:
        across *= 2
    return across, chips // across


def send(value, target):
    dev_count, tp = lax.axis_size("ep"), lax.axis_size("tp")
    pairs = []
    for i in range(dev_count):
        for j in range(tp):
            a, b = target(i, j)
            pairs.append((i * tp + j, a * tp + b))
    return lax.ppermute(value, ("ep", "tp"), pairs)


def send_z(value, k, across):
    return send(value, lambda i, j: (i ^ (2 * across * k), j))


def send_core(value):
    return send(value, lambda i, j: (i ^ 1, j))


def send_x(value, k):
    return send(value, lambda i, j: (i ^ (2 * k), j))


def send_y(value, k):
    return send(value, lambda i, j: (i, j ^ k))


def send_first(value, k):
    return send(value, lambda i, j: (i, j ^ k) if i % 2 else (i ^ (2 * k), j))


def send_last(value, k):
    return send(value, lambda i, j: (i ^ (2 * k), j) if i % 2 else (i, j ^ k))


def xor_blocks(value, axis, index):
    size = value.shape[axis]
    bit = 1
    while bit < size:
        shape = value.shape
        split = shape[:axis] + (size // (2 * bit), 2, bit) + shape[axis + 1 :]
        pairs = value.reshape(split)
        turned = jnp.flip(pairs, axis + 1)
        value = jnp.where((index & bit) > 0, turned, pairs).reshape(shape)
        bit *= 2
    return value


def params():
    return pltpu.CompilerParams(vmem_limit_bytes=VMEM_BYTES)


def whole_spec(shape):
    return pl.BlockSpec(shape, lambda *_: (0,) * len(shape))


def selector(pos_ref, h, cap, experts, tokens):
    slots = lax.broadcasted_iota(jnp.int32, (cap, tokens), 0).astype(F32)
    parts = [
        jnp.where(pos_ref[h, 0, e : e + 1, :] == slots, 1.0, 0.0).astype(F32) for e in range(experts)
    ]
    return jnp.concatenate(parts, axis=0).astype(BF)


def pick_rows(units, pos, start, cap):
    n = len(units)
    group, tokens, width = units[0].shape
    experts = pos.shape[2]

    def body(*refs):
        pos_ref, ins, outs = refs[0], refs[1 : 1 + n], refs[1 + n :]
        for h in range(n):
            chosen = selector(pos_ref, h, cap, experts, tokens)
            rows = jnp.dot(chosen, ins[h][0], preferred_element_type=F32).astype(BF)
            for e in range(experts):
                outs[e][h, 0] = rows[e * cap : (e + 1) * cap]

    return pl.pallas_call(
        body,
        grid=(group,),
        in_specs=[pl.BlockSpec((n, 1, experts, tokens), lambda z: (0, z + start, 0, 0))]
        + [pl.BlockSpec((1, tokens, width), lambda z: (z, 0, 0))] * n,
        out_specs=[pl.BlockSpec((n, 1, cap, width), lambda z: (0, z, 0, 0))] * experts,
        out_shape=[jax.ShapeDtypeStruct((n, group, cap, width), BF)] * experts,
        compiler_params=params(),
        cost_estimate=pl.CostEstimate(
            flops=2 * group * n * experts * cap * tokens * width,
            bytes_accessed=2 * group * n * width * (tokens + experts * cap),
            transcendentals=0,
        ),
        name="pick_rows",
    )(pos, *units)


def spread_rows(sources, pos, start, group, cap, width):
    n, _, experts, tokens = pos.shape

    def body(*refs):
        pos_ref, ins, outs = refs[0], refs[1 : 1 + experts], refs[1 + experts :]
        for h in range(n):
            chosen = selector(pos_ref, h, cap, experts, tokens)
            rows = jnp.concatenate(
                [ref[(0,) * len(prefix) + (h, 0)] for ref, (_, prefix) in zip(ins, sources)], axis=0
            )
            dense = lax.dot_general(chosen, rows, (((0,), (0,)), ((), ())), preferred_element_type=F32)
            outs[h][0] = dense.astype(BF)

    def spec(prefix):
        return pl.BlockSpec((1,) * len(prefix) + (n, 1, cap, width), lambda z: prefix + (0, z, 0, 0))

    return pl.pallas_call(
        body,
        grid=(group,),
        in_specs=[pl.BlockSpec((n, 1, experts, tokens), lambda z: (0, z + start, 0, 0))]
        + [spec(prefix) for _, prefix in sources],
        out_specs=[pl.BlockSpec((1, tokens, width), lambda z: (z, 0, 0))] * n,
        out_shape=[jax.ShapeDtypeStruct((group, tokens, width), BF)] * n,
        compiler_params=params(),
        cost_estimate=pl.CostEstimate(
            flops=2 * group * n * experts * cap * tokens * width,
            bytes_accessed=2 * group * n * width * (tokens + experts * cap),
            transcendentals=0,
        ),
        name="spread_rows",
    )(pos, *[array for array, _ in sources])


def assemble(place, pieces, groups, finish, extra, extra_specs, model_width, name):
    n = len(pieces[0][0])
    _, _, cap, width = pieces[0][0][0].shape
    depth = sum(len(g) for g in groups)
    count = len(groups) * 2 * n

    def body(place_ref, *refs):
        ins, more, out_ref = refs[:count], refs[count:-1], refs[-1]
        z = pl.program_id(0)
        core, col = place_ref[0], place_ref[1]

        def fill(g):
            for cr in range(2):
                kind = core ^ cr
                for f in range(n):
                    ref = ins[(g * 2 + cr) * n + f]
                    for h in range(n):
                        x = jnp.where(kind == 0, h, f)
                        y = jnp.where(kind == 0, f, h) ^ col
                        lanes = pl.ds(pl.multiple_of(y * width, LANES), width)
                        out_ref[0, cr * n + x, :, lanes] = ref[h, 0]

        for g, members in enumerate(groups):
            if len(groups) == 1:
                fill(g)
            else:
                pl.when(jnp.logical_and(z >= members[0], z <= members[-1]))(functools.partial(fill, g))
        for b in range(2 * n):
            out_ref[0, b] = finish(b, out_ref[0, b].astype(F32), *more)

    def piece_spec(members):
        first, last = members[0], members[-1]
        return pl.BlockSpec(
            (n, 1, cap, width), lambda z, *_: (0, jnp.clip(z, first, last) - first, 0, 0)
        )

    in_specs = [piece_spec(members) for members in groups for _ in range(2 * n)]
    flat = [piece for group in pieces for side in group for piece in side]
    return pl.pallas_call(
        body,
        grid_spec=pltpu.PrefetchScalarGridSpec(
            num_scalar_prefetch=1,
            grid=(depth,),
            in_specs=in_specs + extra_specs,
            out_specs=pl.BlockSpec((1, 2 * n, cap, model_width), lambda z, *_: (z, 0, 0, 0)),
        ),
        out_shape=jax.ShapeDtypeStruct((depth, 2 * n, cap, model_width), BF),
        compiler_params=params(),
        cost_estimate=pl.CostEstimate(
            flops=10 * depth * 2 * n * cap * model_width,
            bytes_accessed=4 * depth * 2 * n * cap * model_width,
            transcendentals=0,
        ),
        name=name,
    )(place, *flat, *extra)


def column_product(place, terms, scale, groups, depth, n, cap, width, name):
    count = len(terms)
    units = terms[0][0].shape[1]

    def where_to(y, b, place_ref):
        cr, x = b // n, b % n
        kind = place_ref[0] ^ cr
        y_rel = y ^ place_ref[1]
        return cr, jnp.where(kind == 0, y_rel, x), jnp.where(kind == 0, x, y_rel)

    def body(place_ref, *refs):
        total = None
        for i in range(count):
            left = refs[2 * i][...].reshape(depth * cap, units)
            term = jnp.dot(left, refs[2 * i + 1][...], preferred_element_type=F32)
            total = term if total is None else total + term
        rest = refs[2 * count :]
        if scale is not None:
            total = total * rest[0][...].reshape(depth * cap, LANES)[:, :1]
            rest = rest[1:]
        rows = total.astype(BF).reshape(depth, cap, width)
        for ref, members in zip(rest, groups):
            ref[0, 0, 0] = rows[members[0] : members[-1] + 1]

    left_spec = pl.BlockSpec((depth, 1, cap, units), lambda y, b, *_: (0, b, 0, 0))
    in_specs, args = [], []
    for left, right in terms:
        in_specs += [left_spec, pl.BlockSpec((units, width), lambda y, b, *_: (0, y))]
        args += [left.reshape(depth, 2 * n, cap, units), right]
    if scale is not None:
        in_specs.append(pl.BlockSpec((depth, 1, cap, LANES), lambda y, b, *_: (0, b, 0, 0)))
        args.append(scale)
    return pl.pallas_call(
        body,
        grid_spec=pltpu.PrefetchScalarGridSpec(
            num_scalar_prefetch=1,
            grid=(n, 2 * n),
            in_specs=in_specs,
            out_specs=[
                pl.BlockSpec(
                    (1, 1, 1, len(members), cap, width),
                    lambda y, b, place_ref: where_to(y, b, place_ref) + (0, 0, 0),
                )
                for members in groups
            ],
        ),
        out_shape=[
            jax.ShapeDtypeStruct((2, n, n, len(members), cap, width), BF) for members in groups
        ],
        compiler_params=params(),
        cost_estimate=pl.CostEstimate(
            flops=2 * count * depth * 2 * n * cap * units * width * n,
            bytes_accessed=2 * count * (units * width * n + depth * 2 * n * cap * units)
            + 2 * depth * 2 * n * cap * width * n,
            transcendentals=0,
        ),
        name=name,
    )(place, *args)


def own_selector(pos_ref, b, cap, tokens):
    slots = lax.broadcasted_iota(jnp.int32, (cap, tokens), 0).astype(F32)
    return jnp.where(pos_ref[0, b] == slots, 1.0, 0.0).astype(BF)


def row_sums(active, down_head, pos_own, weight_parts, labels, depth, n, cap):
    units = active.shape[1]
    tokens = pos_own.shape[-1]

    def body(active_ref, head_ref, pos_ref, weight_ref, out_ref, scale_ref):
        for b in range(2 * n):
            chosen = own_selector(pos_ref, b, cap, tokens)
            parts = lax.dot_general(
                chosen, weight_ref[0, b], (((1,), (1,)), ((), ())), preferred_element_type=F32
            )
            scale = parts[:, 0:1] + parts[:, 1:2] + parts[:, 2:3]
            scale_ref[0, b] = jnp.broadcast_to(scale, (cap, LANES))
            rows = jnp.dot(active_ref[0, b], head_ref[...], preferred_element_type=F32) * scale
            high = rows.astype(BF)
            low = (rows - high.astype(F32)).astype(BF)
            dense = lax.dot_general(
                high, chosen, (((0,), (0,)), ((), ())), preferred_element_type=F32
            ) + lax.dot_general(low, chosen, (((0,), (0,)), ((), ())), preferred_element_type=F32)
            out_ref[0, b] = dense[0:labels] + dense[8 : 8 + labels]

    return pl.pallas_call(
        body,
        grid=(depth,),
        in_specs=[
            pl.BlockSpec((1, 2 * n, cap, units), lambda z: (z, 0, 0, 0)),
            whole_spec((units, LANES)),
            pl.BlockSpec((1, 2 * n, 1, tokens), lambda z: (z, 0, 0, 0)),
            pl.BlockSpec((1, 2 * n, 16, tokens), lambda z: (z, 0, 0, 0)),
        ],
        out_specs=[
            pl.BlockSpec((1, 2 * n, labels, tokens), lambda z: (z, 0, 0, 0)),
            pl.BlockSpec((1, 2 * n, cap, LANES), lambda z: (z, 0, 0, 0)),
        ],
        out_shape=[
            jax.ShapeDtypeStruct((depth, 2 * n, labels, tokens), F32),
            jax.ShapeDtypeStruct((depth, 2 * n, cap, LANES), F32),
        ],
        compiler_params=params(),
        cost_estimate=pl.CostEstimate(
            flops=2 * depth * 2 * n * cap * units * LANES,
            bytes_accessed=2 * depth * 2 * n * cap * (units + 256),
            transcendentals=0,
        ),
        name="row_sums",
    )(active.reshape(depth, 2 * n, cap, units), down_head, pos_own, weight_parts)


def gather_rows(value, pos, groups, across, cap, column=None):
    depth = sum(len(g) for g in groups)
    n = across
    if column is None:
        column = [value] + [send_z(value, k, across) for k in range(1, depth)]
    pieces = []
    for members in groups:
        stacked = jnp.stack([column[k] for k in members])
        units = [stacked] + [send_first(stacked, k) for k in range(1, n)]
        rows = pick_rows(units, pos, members[0], cap)
        here, other = [], []
        for f in range(n):
            same, cross = rows[2 * f], rows[2 * f + 1]
            if f > 0:
                cross = send_last(cross, f)
                same = send_last(same, f)
            here.append(same)
            other.append(send_core(cross))
        pieces.append([here, other])
    return pieces


def return_rows(rows, pos, groups, across, cap):
    n = across
    width = rows[0].shape[-1]
    column = {}
    for g in reversed(range(len(groups))):
        members = groups[g]
        mine = rows[g]
        crossed = send_core(mine[1])
        sources = [(mine, (0, 0)), (crossed, (0,))]
        for f in range(1, n):
            sources += [(send_last(mine[0, f], f), ()), (send_last(crossed[f], f), ())]
        dense = spread_rows(sources, pos, members[0], len(members), cap, width)
        total = dense[0].astype(F32)
        for h in range(1, n):
            total = total + send_first(dense[h], h).astype(F32)
        for i, k in enumerate(members):
            column[k] = total[i]
    result = column[0]
    for k in sorted(column, reverse=True):
        if k > 0:
            result = result + send_z(column[k].astype(BF), k, across).astype(F32)
    return result


def sum_all(value):
    step = 1
    while step < lax.axis_size("ep"):
        value = value + send(value, lambda i, j: (i ^ step, j))
        step *= 2
    step = 1
    while step < lax.axis_size("tp"):
        value = value + send_y(value, step)
        step *= 2
    return value


def split_bf(value, parts):
    pieces = []
    for _ in range(parts):
        piece = value.astype(BF)
        pieces.append(piece)
        value = value - piece.astype(F32)
    return pieces


def shards(
    hidden_in,
    norm_gain,
    expert_ids,
    routing_weight,
    labels,
    grad_later,
    head_weight,
    gate_weight,
    up_weight,
    down_weight,
):
    dev_count = lax.axis_size("ep")
    n = lax.axis_size("tp")
    row, col = lax.axis_index("ep"), lax.axis_index("tp")
    core = row & 1
    across, depth = ring_sizes(dev_count)
    if across != n:
        raise ValueError("x and y differ")
    tok_count, width = hidden_in.shape
    top_count = expert_ids.shape[1]
    model_width = gate_weight.shape[1]
    unit_rows = gate_weight.shape[0]
    local_count = unit_rows * n // FF
    expert_count = local_count * dev_count
    capacity = tok_count * top_count * 3 // (2 * expert_count)
    cap = -(-capacity // 16) * 16
    row_count = dev_count * cap
    label_count = head_weight.shape[1]
    place = jnp.stack([core, col]).astype(jnp.int32)
    two = [tuple(range(depth // 2)), tuple(range(depth // 2, depth))]
    one = [tuple(range(depth))]

    def expert_of(ep_index, tp_index):
        return ep_index * local_count + tp_index * unit_rows // FF

    spare = -(2 * top_count + 1) % 8
    meta = jnp.concatenate(
        [
            expert_ids.T.astype(F32),
            routing_weight.T,
            labels.astype(F32)[None, :],
            jnp.zeros((spare, tok_count), F32),
        ]
    )
    meta = jnp.stack([meta] + [send_z(meta, k, across) for k in range(1, depth)])
    meta = jnp.stack([meta] + [send_x(meta, k) for k in range(1, n)], axis=1)
    meta = jnp.stack([meta, send_core(meta)], axis=1)

    feature_rows = jnp.concatenate(
        [
            norm_gain[None, :],
            head_weight.astype(F32).T,
            jnp.zeros((-(1 + label_count) % 8, width), F32),
        ]
    )
    own_gain, own_head = feature_rows[0], feature_rows[1 : 1 + label_count]
    all_features = jnp.stack([feature_rows] + [send_y(feature_rows, j) for j in range(1, n)], axis=1)
    all_features = xor_blocks(all_features, 1, col).reshape(feature_rows.shape[0], model_width)

    hidden_column = [hidden_in] + [send_z(hidden_in, k, across) for k in range(1, depth)]

    spot = jnp.arange(tok_count, dtype=jnp.int32)
    earlier = (spot[:, None] < spot[None, :]).astype(BF)

    def positions(ids, experts):
        member = jnp.stack([jnp.sum((ids == e.astype(F32)).astype(F32), axis=-2) for e in experts], axis=-2)
        before = lax.dot_general(
            member.astype(BF), earlier, (((member.ndim - 1,), (0,)), ((), ())), preferred_element_type=F32
        )
        return jnp.where(member > 0, before, -1.0)

    ids = meta[..., :top_count, :]
    near = [expert_of(row, col), expert_of(row ^ 1, col)]
    for f in range(1, n):
        far_row = jnp.where(core == 0, row, row ^ (2 * f))
        far_col = jnp.where(core == 0, col ^ f, col)
        near += [expert_of(far_row, far_col), expert_of(far_row ^ 1, far_col)]
    unit_ids = jnp.stack([jnp.where(core == 0, ids[:, 0, h], ids[:, 0, 0]) for h in range(n)])
    pos = positions(unit_ids, near)
    blocks = ids.reshape(depth, 2 * n, top_count, tok_count)
    pos_own = positions(blocks, [expert_of(row, col)])
    named_own = (blocks == expert_of(row, col).astype(F32)).astype(F32)
    weights = meta[..., top_count : 2 * top_count, :].reshape(blocks.shape)
    weight_own = jnp.sum(named_own * weights, axis=-2, keepdims=True)
    blank = jnp.zeros((depth, 2 * n, 13, tok_count), BF)
    weight_parts = jnp.concatenate(split_bf(weight_own, 3) + [blank], axis=2)
    label_all = meta[..., 2 * top_count, :]

    hidden_wide = hidden_in.astype(F32)
    own_squares = jnp.sum(hidden_wide * hidden_wide, axis=1)
    squares = own_squares
    for j in range(1, n):
        squares = squares + send_y(own_squares, j)
    inv_rms = lax.rsqrt(squares / model_width + EPS)[:, None]

    head_pair = jnp.concatenate([all_features[1:], jnp.zeros((1, model_width), F32)])
    head_pad = jnp.concatenate(
        [head_pair, head_pair, jnp.zeros((LANES - 16, model_width), F32)]
    ).astype(BF)
    down_head = lax.dot_general(
        down_weight, head_pad, (((1,), (1,)), ((), ())), preferred_element_type=F32
    )
    high = down_head.astype(BF)
    lane = lax.broadcasted_iota(jnp.int32, down_head.shape, 1)
    down_head = jnp.where(lane < 8, high, (down_head - high.astype(F32)).astype(BF))

    pieces = gather_rows(hidden_in, pos, two, across, cap, hidden_column)

    def normed(b, value, features_ref):
        rms = lax.rsqrt(jnp.sum(value * value, axis=1, keepdims=True) / model_width + EPS)
        return (value * rms * features_ref[0:1, :]).astype(BF)

    received = assemble(
        place, pieces, two, normed, [all_features], [whole_spec(all_features.shape)], model_width, "normed_rows"
    ).reshape(row_count, model_width)

    later_in = lax.optimization_barrier([grad_later] + hidden_column)[0]
    later = gather_rows(later_in, pos, one, across, cap)

    def against(left, right):
        return lax.dot_general(left, right, (((1,), (1,)), ((), ())), preferred_element_type=F32)

    def over_rows(left, right):
        return lax.dot_general(left, right, (((0,), (0,)), ((), ())), preferred_element_type=F32).astype(BF)

    gate_pre = against(received, gate_weight)
    up_pre = against(received, up_weight)
    sigma = jax.nn.sigmoid(gate_pre)
    active = (gate_pre * sigma * up_pre).astype(BF)

    logits, scale = row_sums(active, down_head, pos_own, weight_parts, label_count, depth, n, cap)
    own_logits = lax.dot_general(
        own_head.astype(BF), hidden_in, (((1,), (1,)), ((), ())), preferred_element_type=F32
    )

    def turn(value):
        value = value.reshape((depth, 2, n) + value.shape[-2:])
        value = xor_blocks(value, 0, row // (2 * across))
        value = xor_blocks(value, 1, core)
        return xor_blocks(value, 2, (row // 2) & (across - 1))

    block = jnp.arange(depth * 2 * n).reshape(depth, 2 * n)
    logits = logits + jnp.where((block == 0)[..., None, None], own_logits, 0.0)
    logits = turn(sum_all(turn(logits)))
    classes = (label_all[..., None, :] == jnp.arange(label_count, dtype=F32)[:, None]).astype(F32)
    powers = jnp.exp(logits)
    totals = jnp.sum(powers, axis=-2, keepdims=True)
    d_logits = (powers / totals - classes) * LOSS_SCALE
    token_loss = jnp.log(totals[0, 0, 0, 0]) - jnp.sum(logits[0, 0, 0] * classes[0, 0, 0], axis=0)

    d_parts = jnp.concatenate(
        split_bf(d_logits.reshape(depth, 2 * n, label_count, tok_count), 2)
        + [weight_parts[:, :, : 16 - 2 * label_count]],
        axis=2,
    )

    def gradient_rows(b, value, features_ref, pos_ref, parts_ref):
        chosen = own_selector(pos_ref, b, cap, tok_count)
        parts = lax.dot_general(
            chosen, parts_ref[0, b], (((1,), (1,)), ((), ())), preferred_element_type=F32
        )
        for k in range(label_count):
            d_logit = parts[:, k : k + 1] + parts[:, label_count + k : label_count + k + 1]
            value = value + d_logit * features_ref[1 + k : 2 + k, :]
        first = 2 * label_count
        weight = parts[:, first : first + 1] + parts[:, first + 1 : first + 2] + parts[:, first + 2 : first + 3]
        return (value.astype(BF).astype(F32) * weight).astype(BF)

    grads_in = assemble(
        place,
        later,
        one,
        gradient_rows,
        [all_features, pos_own, d_parts],
        [
            whole_spec(all_features.shape),
            pl.BlockSpec((1, 2 * n, 1, tok_count), lambda z, *_: (z, 0, 0, 0)),
            pl.BlockSpec((1, 2 * n, 16, tok_count), lambda z, *_: (z, 0, 0, 0)),
        ],
        model_width,
        "gradient_rows",
    ).reshape(row_count, model_width)

    d_active = against(grads_in, down_weight)
    d_gate = (d_active * up_pre * sigma * (1.0 + gate_pre * (1.0 - sigma))).astype(BF)
    d_up = (d_active * gate_pre * sigma).astype(BF)

    d_rows = column_product(
        place, [(d_gate, gate_weight), (d_up, up_weight)], None, two, depth, n, cap, width, "d_rows"
    )
    d_normed = return_rows(d_rows, pos, two, across, cap)
    out_rows = column_product(
        place, [(active, down_weight)], scale, one, depth, n, cap, width, "out_rows"
    )
    mixed = return_rows(out_rows, pos, one, across, cap)

    grad_down = over_rows(active, grads_in)
    grad_gate = over_rows(d_gate, received)
    grad_up = over_rows(d_up, received)

    outcome = (hidden_wide + mixed).astype(BF)
    d_outcome = lax.dot_general(
        d_logits[0, 0, 0], own_head, (((0,), (0,)), ((), ())), precision=EXACT
    ) + grad_later.astype(F32)
    d_scaled = d_normed * own_gain[None, :]
    products = jnp.sum(d_scaled * hidden_wide, axis=1)
    slope = products
    for j in range(1, n):
        slope = slope + send_y(products, j)
    slope = slope[:, None] / model_width
    d_hidden = inv_rms * d_scaled - hidden_wide * (inv_rms * inv_rms * inv_rms) * slope
    grad_input = (d_outcome + d_hidden).astype(BF)
    return token_loss, outcome, grad_input, grad_gate, grad_up, grad_down


def solution(mesh):
    in_specs = (
        P("ep", "tp"),
        P("tp"),
        P("ep", None),
        P("ep", None),
        P("ep"),
        P("ep", "tp"),
        P("tp", None),
        P(("ep", "tp"), None),
        P(("ep", "tp"), None),
        P(("ep", "tp"), None),
    )
    out_specs = (
        P("ep"),
        P("ep", "tp"),
        P("ep", "tp"),
        P(("ep", "tp"), None),
        P(("ep", "tp"), None),
        P(("ep", "tp"), None),
    )
    return jax.shard_map(shards, mesh=mesh, in_specs=in_specs, out_specs=out_specs, check_vma=False)
```

```python
import functools

import jax
import jax.numpy as jnp
from jax import lax
from jax.experimental import pallas as pl
from jax.experimental.pallas import tpu as pltpu
from jax.sharding import PartitionSpec as P

FF = 768

EPS = 1e-06
LOSS_SCALE = 64.0
BF = jnp.bfloat16
F32 = jnp.float32
EXACT = lax.Precision.HIGHEST
VMEM_BYTES = 24 * 1024 * 1024
LANES = 128


def ring_sizes(dev_count):
    chips = dev_count // 2
    across = 1
    while across * across * 4 <= chips:
        across *= 2
    return across, chips // across


def send(value, target):
    dev_count, tp = lax.axis_size("ep"), lax.axis_size("tp")
    pairs = []
    for i in range(dev_count):
        for j in range(tp):
            a, b = target(i, j)
            pairs.append((i * tp + j, a * tp + b))
    return lax.ppermute(value, ("ep", "tp"), pairs)


def send_z(value, k, across):
    return send(value, lambda i, j: (i ^ (2 * across * k), j))


def send_core(value):
    return send(value, lambda i, j: (i ^ 1, j))


def send_x(value, k):
    return send(value, lambda i, j: (i ^ (2 * k), j))


def send_y(value, k):
    return send(value, lambda i, j: (i, j ^ k))


def send_first(value, k):
    return send(value, lambda i, j: (i, j ^ k) if i % 2 else (i ^ (2 * k), j))


def send_last(value, k):
    return send(value, lambda i, j: (i ^ (2 * k), j) if i % 2 else (i, j ^ k))


def z_gather(value, depth, n):
    column = {0: value}
    bit = depth // 2
    while bit:
        for k in list(column):
            column[k ^ bit] = send_z(column[k], bit, n)
        bit //= 2
    return [column[k] for k in range(depth)]


def z_reduce(column, n):
    blocks = dict(enumerate(column))
    bit = 1
    while bit < len(column):
        for k in sorted(blocks, reverse=True):
            if k & bit:
                blocks[k ^ bit] = blocks[k ^ bit] + send_z(blocks.pop(k).astype(BF), bit, n).astype(F32)
        bit *= 2
    return blocks[0]


def xor_blocks(value, axis, index):
    size = value.shape[axis]
    bit = 1
    while bit < size:
        shape = value.shape
        split = shape[:axis] + (size // (2 * bit), 2, bit) + shape[axis + 1 :]
        pairs = value.reshape(split)
        turned = jnp.flip(pairs, axis + 1)
        value = jnp.where((index & bit) > 0, turned, pairs).reshape(shape)
        bit *= 2
    return value


def params():
    return pltpu.CompilerParams(vmem_limit_bytes=VMEM_BYTES)


def whole_spec(shape):
    return pl.BlockSpec(shape, lambda *_: (0,) * len(shape))


def selector(pos_ref, h, z, cap, experts, tokens):
    slots = lax.broadcasted_iota(jnp.int32, (cap, tokens), 0).astype(F32)
    parts = [
        jnp.where(pos_ref[h, z, e : e + 1, :] == slots, 1.0, 0.0).astype(F32) for e in range(experts)
    ]
    return jnp.concatenate(parts, axis=0).astype(BF)


def pick_rows(units, after, pos, start, cap):
    n, _, experts, tokens = pos.shape
    stacked = not isinstance(units[0], (list, tuple))
    group = units[0].shape[0] if stacked else len(units)
    flat = list(units) if stacked else [unit for at_z in units for unit in at_z]
    width = flat[0].shape[-1]

    def body(pos_ref, *refs):
        ins, outs = refs[: len(flat)], refs[-experts:]
        for z in range(group):
            for h in range(n):
                chosen = selector(pos_ref, h, start + z, cap, experts, tokens)
                unit = ins[h][z] if stacked else ins[z * n + h][...]
                rows = jnp.dot(chosen, unit, preferred_element_type=F32).astype(BF)
                for e in range(experts):
                    outs[e][h, z] = rows[e * cap : (e + 1) * cap]

    vmem = pl.BlockSpec(memory_space=pltpu.VMEM)
    return pl.pallas_call(
        body,
        in_specs=[vmem] * (1 + len(flat)) + [pl.BlockSpec(memory_space=pl.ANY)] * len(after),
        out_specs=[vmem] * experts,
        out_shape=[jax.ShapeDtypeStruct((n, group, cap, width), BF)] * experts,
        compiler_params=params(),
        cost_estimate=pl.CostEstimate(
            flops=2 * group * n * experts * cap * tokens * width,
            bytes_accessed=2 * group * n * width * (tokens + experts * cap),
            transcendentals=0,
        ),
        name="pick_rows",
    )(pos, *flat, *after)


def spread_rows(sources, after, pos, start, group, cap, width):
    n, _, experts, tokens = pos.shape

    def body(*refs):
        pos_ref, ins, outs = refs[0], refs[1 : 1 + experts], refs[-n:]
        for h in range(n):
            chosen = selector(pos_ref, h, 0, cap, experts, tokens)
            rows = jnp.concatenate(
                [ref[(0,) * len(prefix) + (h, 0)] for ref, (_, prefix) in zip(ins, sources)], axis=0
            )
            dense = lax.dot_general(chosen, rows, (((0,), (0,)), ((), ())), preferred_element_type=F32)
            outs[h][0] = dense.astype(BF)

    def spec(prefix):
        return pl.BlockSpec((1,) * len(prefix) + (n, 1, cap, width), lambda z: prefix + (0, z, 0, 0))

    return pl.pallas_call(
        body,
        grid=(group,),
        in_specs=[pl.BlockSpec((n, 1, experts, tokens), lambda z: (0, z + start, 0, 0))]
        + [spec(prefix) for _, prefix in sources]
        + [pl.BlockSpec(memory_space=pl.ANY)] * len(after),
        out_specs=[pl.BlockSpec((1, tokens, width), lambda z: (z, 0, 0))] * n,
        out_shape=[jax.ShapeDtypeStruct((group, tokens, width), BF)] * n,
        compiler_params=params(),
        cost_estimate=pl.CostEstimate(
            flops=2 * group * n * experts * cap * tokens * width,
            bytes_accessed=2 * group * n * width * (tokens + experts * cap),
            transcendentals=0,
        ),
        name="spread_rows",
    )(pos, *[array for array, _ in sources], *after)


def assemble(place, pieces, groups, finish, extra, extra_specs, after, model_width, name):
    n = len(pieces[0][0])
    _, _, cap, width = pieces[0][0][0].shape
    depth = sum(len(g) for g in groups)
    count = len(groups) * 2 * n

    def body(place_ref, *refs):
        ins, more, out_ref = refs[:count], refs[count : count + len(extra)], refs[-1]
        z = pl.program_id(0)
        core, col = place_ref[0], place_ref[1]

        def fill(g):
            for cr in range(2):
                kind = core ^ cr
                for f in range(n):
                    ref = ins[(g * 2 + cr) * n + f]
                    for h in range(n):
                        x = jnp.where(kind == 0, h, f)
                        y = jnp.where(kind == 0, f, h) ^ col
                        lanes = pl.ds(pl.multiple_of(y * width, LANES), width)
                        out_ref[0, cr * n + x, :, lanes] = ref[h, 0]

        for g, members in enumerate(groups):
            if len(groups) == 1:
                fill(g)
            else:
                pl.when(jnp.logical_and(z >= members[0], z <= members[-1]))(functools.partial(fill, g))
        finish(out_ref, *more)

    def piece_spec(members):
        first, last = members[0], members[-1]
        return pl.BlockSpec(
            (n, 1, cap, width), lambda z, *_: (0, jnp.clip(z, first, last) - first, 0, 0)
        )

    in_specs = [piece_spec(members) for members in groups for _ in range(2 * n)]
    flat = [piece for group in pieces for side in group for piece in side]
    return pl.pallas_call(
        body,
        grid_spec=pltpu.PrefetchScalarGridSpec(
            num_scalar_prefetch=1,
            grid=(depth,),
            in_specs=in_specs + extra_specs + [pl.BlockSpec(memory_space=pl.ANY)] * len(after),
            out_specs=pl.BlockSpec((1, 2 * n, cap, model_width), lambda z, *_: (z, 0, 0, 0)),
        ),
        out_shape=jax.ShapeDtypeStruct((depth, 2 * n, cap, model_width), BF),
        compiler_params=params(),
        cost_estimate=pl.CostEstimate(
            flops=10 * depth * 2 * n * cap * model_width,
            bytes_accessed=4 * depth * 2 * n * cap * model_width,
            transcendentals=0,
        ),
        name=name,
    )(place, *flat, *extra, *after)


def column_product(place, terms, scale, after, groups, depth, n, cap, width, name):
    count = len(terms)
    units = terms[0][0].shape[1]

    def where_to(y, b, place_ref):
        cr, x = b // n, b % n
        kind = place_ref[0] ^ cr
        y_rel = y ^ place_ref[1]
        return cr, jnp.where(kind == 0, y_rel, x), jnp.where(kind == 0, x, y_rel)

    def body(place_ref, *refs):
        total = None
        for i in range(count):
            left = refs[2 * i][...].reshape(depth * cap, units)
            term = jnp.dot(left, refs[2 * i + 1][...], preferred_element_type=F32)
            total = term if total is None else total + term
        rest = refs[2 * count :]
        rows = total.reshape(depth, cap, width)
        if scale is not None:
            rows = jnp.stack(
                [
                    rows[z] * row_weight(own_selector(rest[0][z, 0], cap), rest[1][z, 0])
                    for z in range(depth)
                ]
            )
            rest = rest[2:]
        rows = rows.astype(BF)
        rest = rest[len(after) :]
        for ref, members in zip(rest, groups):
            ref[0, 0, 0] = rows[members[0] : members[-1] + 1]

    left_spec = pl.BlockSpec((depth, 1, cap, units), lambda y, b, *_: (0, b, 0, 0))
    in_specs, args = [], []
    for left, right in terms:
        in_specs += [left_spec, pl.BlockSpec((units, width), lambda y, b, *_: (0, y))]
        args += [left.reshape(depth, 2 * n, cap, units), right]
    if scale is not None:
        in_specs += [
            pl.BlockSpec((depth, 1) + array.shape[2:], lambda y, b, *_: (0, b, 0, 0)) for array in scale
        ]
        args += scale
    in_specs += [pl.BlockSpec(memory_space=pl.ANY)] * len(after)
    args += after
    return pl.pallas_call(
        body,
        grid_spec=pltpu.PrefetchScalarGridSpec(
            num_scalar_prefetch=1,
            grid=(n, 2 * n),
            in_specs=in_specs,
            out_specs=[
                pl.BlockSpec(
                    (1, 1, 1, len(members), cap, width),
                    lambda y, b, place_ref: where_to(y, b, place_ref) + (0, 0, 0),
                )
                for members in groups
            ],
        ),
        out_shape=[
            jax.ShapeDtypeStruct((2, n, n, len(members), cap, width), BF) for members in groups
        ],
        compiler_params=params(),
        cost_estimate=pl.CostEstimate(
            flops=2 * count * depth * 2 * n * cap * units * width * n,
            bytes_accessed=2 * count * (units * width * n + depth * 2 * n * cap * units)
            + 2 * depth * 2 * n * cap * width * n,
            transcendentals=0,
        ),
        name=name,
    )(place, *args)


def own_selector(pos, cap):
    slots = lax.broadcasted_iota(jnp.int32, (cap, pos.shape[1]), 0).astype(F32)
    return jnp.where(pos == slots, 1.0, 0.0).astype(BF)


def wide_selector(pos_ref, blocks, cap):
    tokens = pos_ref.shape[-1]
    slots = lax.broadcasted_iota(jnp.int32, (blocks * cap, tokens), 0).astype(F32)
    parts = []
    for b in range(blocks):
        pos = pos_ref[0, b]
        parts.append(jnp.where(jnp.where(pos < 0, pos, pos + b * cap) == slots, 1.0, 0.0))
    return jnp.concatenate(parts, axis=1).astype(BF)


def row_weight(chosen, parts):
    picked = lax.dot_general(chosen, parts, (((1,), (1,)), ((), ())), preferred_element_type=F32)
    return picked[:, 0:1] + picked[:, 1:2] + picked[:, 2:3]


def row_sums(active, down_head, pos_own, weight_own, after, labels, depth, n, cap):
    units = active.shape[1]
    tokens = pos_own.shape[-1]

    def body(active_ref, head_ref, pos_ref, weight_ref, *rest):
        out_ref = rest[-1]
        chosen = wide_selector(pos_ref, 2 * n, cap)
        rows = active_ref[0].reshape(2 * n * cap, units)
        sums = lax.dot_general(head_ref[...], rows, (((1,), (1,)), ((), ())), preferred_element_type=F32)
        high = sums.astype(BF)
        low = (sums - high.astype(F32)).astype(BF)
        dense = jnp.dot(high, chosen, preferred_element_type=F32) + jnp.dot(
            low, chosen, preferred_element_type=F32
        )
        for b in range(2 * n):
            own = dense[:, b * tokens : (b + 1) * tokens]
            out_ref[0, b] = (own[0:labels] + own[8 : 8 + labels]) * weight_ref[0, b]

    return pl.pallas_call(
        body,
        grid=(depth,),
        in_specs=[
            pl.BlockSpec((1, 2 * n, cap, units), lambda z: (z, 0, 0, 0)),
            whole_spec(down_head.shape),
            pl.BlockSpec((1, 2 * n, 1, tokens), lambda z: (z, 0, 0, 0)),
            pl.BlockSpec((1, 2 * n, 1, tokens), lambda z: (z, 0, 0, 0)),
        ]
        + [pl.BlockSpec(memory_space=pl.ANY)] * len(after),
        out_specs=pl.BlockSpec((1, 2 * n, labels, tokens), lambda z: (z, 0, 0, 0)),
        out_shape=jax.ShapeDtypeStruct((depth, 2 * n, labels, tokens), F32),
        compiler_params=params(),
        cost_estimate=pl.CostEstimate(
            flops=2 * depth * 2 * n * cap * units * 16,
            bytes_accessed=2 * depth * 2 * n * cap * units,
            transcendentals=0,
        ),
        name="row_sums",
    )(active.reshape(depth, 2 * n, cap, units), down_head, pos_own, weight_own, *after)


def route_rows(units, after, pos, start, cap):
    rows = pick_rows(units, after, pos, start, cap)
    n = pos.shape[0]
    here, other = [], []
    for f in range(n):
        same, cross = rows[2 * f], rows[2 * f + 1]
        if f > 0:
            cross = send_last(cross, f)
            same = send_last(same, f)
        here.append(same)
        other.append(send_core(cross))
    return [here, other], rows


def gather_by_column(column, after, pos, groups, n, cap):
    units = [[value] + [send_first(value, k) for k in range(1, n)] for value in column]
    routed = [
        route_rows([units[k] for k in members], more, pos, members[0], cap)
        for members, more in zip(groups, after)
    ]
    return [pieces for pieces, _ in routed], routed[0][1]


def pick_at_once(column, pos, n, cap):
    column = jnp.stack(column)
    units = [column] + [send_first(column, k) for k in range(1, n)]
    pieces, rows = route_rows(units, [], pos, 0, cap)
    return [pieces], rows


def return_sources(rows, crossed, n):
    sources = [(rows, (0, 0)), (crossed, (0,))]
    for f in range(1, n):
        sources += [(send_last(rows[0, f], f), ()), (send_last(crossed[f], f), ())]
    return sources


def spread_back(rows, crossed, after, pos, start, n, cap):
    group, _, width = rows.shape[3:]
    return spread_rows(return_sources(rows, crossed, n), after, pos, start, group, cap, width)


def first_sum(dense):
    total = dense[0].astype(F32)
    for h in range(1, len(dense)):
        total = total + send_first(dense[h], h).astype(F32)
    return total


def sum_all(value, after, across, depth):
    value = value + send_core(value)
    step = 1
    while step < depth:
        value = value + send_z(value, step, across)
        step *= 2
    value = lax.optimization_barrier([value] + after)[0]
    step = 1
    while step < across:
        value = value + send_x(value, step)
        step *= 2
    step = 1
    while step < lax.axis_size("tp"):
        value = value + send_y(value, step)
        step *= 2
    return value


def split_bf(value, parts):
    pieces = []
    for _ in range(parts):
        piece = value.astype(BF)
        pieces.append(piece)
        value = value - piece.astype(F32)
    return pieces


def shards(
    hidden_in,
    norm_gain,
    expert_ids,
    routing_weight,
    labels,
    grad_later,
    head_weight,
    gate_weight,
    up_weight,
    down_weight,
):
    dev_count = lax.axis_size("ep")
    n = lax.axis_size("tp")
    row, col = lax.axis_index("ep"), lax.axis_index("tp")
    core = row & 1
    across, depth = ring_sizes(dev_count)
    if across != n:
        raise ValueError("x and y differ")
    tok_count, width = hidden_in.shape
    top_count = expert_ids.shape[1]
    model_width = gate_weight.shape[1]
    unit_rows = gate_weight.shape[0]
    local_count = unit_rows * n // FF
    expert_count = local_count * dev_count
    capacity = tok_count * top_count * 3 // (2 * expert_count)
    cap = -(-capacity // 16) * 16
    row_count = dev_count * cap
    label_count = head_weight.shape[1]
    place = jnp.stack([core, col]).astype(jnp.int32)
    two = [tuple(range(depth // 2)), tuple(range(depth // 2, depth))]
    one = [tuple(range(depth))]

    def expert_of(ep_index, tp_index):
        return ep_index * local_count + tp_index * unit_rows // FF

    hidden_column = z_gather(hidden_in, depth, n)

    spare = -(2 * top_count + 1) % 8
    meta = jnp.concatenate(
        [
            expert_ids.T.astype(F32),
            routing_weight.T,
            labels.astype(F32)[None, :],
            jnp.zeros((spare, tok_count), F32),
        ]
    )
    meta = jnp.stack(z_gather(meta, depth, n))
    meta = jnp.stack([meta] + [send_x(meta, k) for k in range(1, n)], axis=1)
    meta = jnp.stack([meta, send_core(meta)], axis=1)

    hidden_wide = hidden_in.astype(F32)
    own_squares = jnp.sum(hidden_wide * hidden_wide, axis=1)
    feature_rows = jnp.concatenate(
        [
            norm_gain[None, :],
            head_weight.astype(F32).T,
            jnp.pad(own_squares[None, :], ((0, 0), (0, width - tok_count))),
            jnp.zeros((-(2 + label_count) % 8, width), F32),
        ]
    )
    own_gain, own_head = feature_rows[0], feature_rows[1 : 1 + label_count]
    all_features = jnp.stack([feature_rows] + [send_y(feature_rows, j) for j in range(1, n)], axis=1)
    squares = jnp.sum(all_features[1 + label_count, :, :tok_count], axis=0)
    inv_rms = lax.rsqrt(squares / model_width + EPS)[:, None]
    all_features = xor_blocks(all_features, 1, col).reshape(feature_rows.shape[0], model_width)

    spot = jnp.arange(tok_count, dtype=jnp.int32)
    earlier = (spot[:, None] < spot[None, :]).astype(BF)

    def positions(ids, experts):
        member = jnp.stack([jnp.sum((ids == e.astype(F32)).astype(F32), axis=-2) for e in experts], axis=-2)
        before = lax.dot_general(
            member.astype(BF), earlier, (((member.ndim - 1,), (0,)), ((), ())), preferred_element_type=F32
        )
        return jnp.where(member > 0, before, -1.0)

    ids = meta[..., :top_count, :]
    near = [expert_of(row, col), expert_of(row ^ 1, col)]
    for f in range(1, n):
        far_row = jnp.where(core == 0, row, row ^ (2 * f))
        far_col = jnp.where(core == 0, col ^ f, col)
        near += [expert_of(far_row, far_col), expert_of(far_row ^ 1, far_col)]
    unit_ids = jnp.stack([jnp.where(core == 0, ids[:, 0, h], ids[:, 0, 0]) for h in range(n)])
    pos = positions(unit_ids, near)
    blocks = ids.reshape(depth, 2 * n, top_count, tok_count)
    pos_own = positions(blocks, [expert_of(row, col)])
    named_own = (blocks == expert_of(row, col).astype(F32)).astype(F32)
    weights = meta[..., top_count : 2 * top_count, :].reshape(blocks.shape)
    weight_own = jnp.sum(named_own * weights, axis=-2, keepdims=True)
    blank = jnp.zeros((depth, 2 * n, 13, tok_count), BF)
    weight_parts = jnp.concatenate(split_bf(weight_own, 3) + [blank], axis=2)
    label_all = meta[..., 2 * top_count, :]

    head_pair = jnp.concatenate(
        [all_features[1 : 1 + label_count], jnp.zeros((8 - label_count, model_width), F32)]
    )
    head_pair = jnp.concatenate([head_pair, head_pair]).astype(BF)
    down_head = lax.dot_general(
        head_pair, down_weight, (((1,), (1,)), ((), ())), preferred_element_type=F32
    )
    high = down_head.astype(BF)
    which = lax.broadcasted_iota(jnp.int32, down_head.shape, 0)
    down_head = jnp.where(which < 8, high, (down_head - high.astype(F32)).astype(BF))

    later_in = lax.optimization_barrier([grad_later, hidden_column[depth // 2]])[0]
    later_column = z_gather(later_in, depth, n)
    pieces, _ = gather_by_column(hidden_column, [[], later_column[depth // 2 : depth // 2 + 1]], pos, two, n, cap)

    def normed(out_ref, features_ref):
        for b in range(2 * n):
            value = out_ref[0, b].astype(F32)
            rms = lax.rsqrt(jnp.sum(value * value, axis=1, keepdims=True) / model_width + EPS)
            out_ref[0, b] = (value * rms * features_ref[0:1, :]).astype(BF)

    received = assemble(
        place,
        pieces,
        two,
        normed,
        [all_features],
        [whole_spec(all_features.shape)],
        [],
        model_width,
        "normed_rows",
    ).reshape(row_count, model_width)
    later, picked_later = pick_at_once(later_column, pos, n, cap)

    def against(left, right):
        return lax.dot_general(left, right, (((1,), (1,)), ((), ())), preferred_element_type=F32)

    def over_rows(left, right):
        return lax.dot_general(left, right, (((0,), (0,)), ((), ())), preferred_element_type=F32).astype(BF)

    gate_pre = against(received, gate_weight)
    up_pre = against(received, up_weight)
    sigma = jax.nn.sigmoid(gate_pre)
    active = (gate_pre * sigma * up_pre).astype(BF)

    logits = row_sums(active, down_head, pos_own, weight_own, list(picked_later[:1]), label_count, depth, n, cap)
    out_rows = column_product(
        place, [(active, down_weight)], [pos_own, weight_parts], list(picked_later[:1]), one, depth, n, cap, width, "out_rows"
    )[0]
    crossed = send_core(out_rows[1])
    out_dense = spread_back(out_rows, crossed, [], pos, 0, n, cap)
    out_column = first_sum(out_dense)
    own_logits = lax.dot_general(
        own_head.astype(BF), hidden_in, (((1,), (1,)), ((), ())), preferred_element_type=F32
    )

    def turn(value):
        value = value.reshape((depth, 2, n) + value.shape[-2:])
        value = xor_blocks(value, 0, row // (2 * across))
        value = xor_blocks(value, 1, core)
        return xor_blocks(value, 2, (row // 2) & (across - 1))

    block = jnp.arange(depth * 2 * n).reshape(depth, 2 * n)
    logits = logits + jnp.where((block == 0)[..., None, None], own_logits, 0.0)
    logits = turn(sum_all(turn(logits), later[0][0] + later[0][1], across, depth))
    classes = (label_all[..., None, :] == jnp.arange(label_count, dtype=F32)[:, None]).astype(F32)
    powers = jnp.exp(logits)
    totals = jnp.sum(powers, axis=-2, keepdims=True)
    d_logits = (powers / totals - classes) * LOSS_SCALE
    token_loss = jnp.log(totals[0, 0, 0, 0]) - jnp.sum(logits[0, 0, 0] * classes[0, 0, 0], axis=0)

    d_parts = jnp.concatenate(
        split_bf(d_logits.reshape(depth, 2 * n, label_count, tok_count), 2)
        + [weight_parts[:, :, : 16 - 2 * label_count]],
        axis=2,
    )

    keys = jnp.concatenate([all_features[1 : 1 + label_count]] * 2)
    keys = jnp.concatenate([keys, jnp.zeros((16 - 2 * label_count, model_width), F32)]).astype(BF)

    def gradient_rows(out_ref, keys_ref, pos_ref, parts_ref):
        chosen = wide_selector(pos_ref, 2 * n, cap)
        parts = jnp.concatenate([parts_ref[0, b] for b in range(2 * n)], axis=1)
        picked = lax.dot_general(chosen, parts, (((1,), (1,)), ((), ())), preferred_element_type=F32)
        first = 2 * label_count
        weight = picked[:, first : first + 1] + picked[:, first + 1 : first + 2] + picked[:, first + 2 : first + 3]
        head_term = jnp.dot(picked.astype(BF), keys_ref[...], preferred_element_type=F32)
        for b in range(2 * n):
            part = slice(b * cap, (b + 1) * cap)
            value = head_term[part] + out_ref[0, b].astype(F32)
            out_ref[0, b] = (value.astype(BF).astype(F32) * weight[part]).astype(BF)

    grads_in = assemble(
        place,
        later,
        one,
        gradient_rows,
        [keys, pos_own, d_parts],
        [
            whole_spec(keys.shape),
            pl.BlockSpec((1, 2 * n, 1, tok_count), lambda z, *_: (z, 0, 0, 0)),
            pl.BlockSpec((1, 2 * n, 16, tok_count), lambda z, *_: (z, 0, 0, 0)),
        ],
        [crossed],
        model_width,
        "gradient_rows",
    ).reshape(row_count, model_width)

    d_active = against(grads_in, down_weight)
    d_gate = (d_active * up_pre * sigma * (1.0 + gate_pre * (1.0 - sigma))).astype(BF)
    d_up = (d_active * gate_pre * sigma).astype(BF)

    d_rows = column_product(
        place, [(d_gate, gate_weight), (d_up, up_weight)], None, list(out_dense[:1]), two, depth, n, cap, width, "d_rows"
    )
    mixed = z_reduce(out_column, n)
    d_column = [None] * depth
    after = []
    for rows, members in reversed(list(zip(d_rows, two))):
        sums = first_sum(spread_back(rows, send_core(rows[1]), after, pos, members[0], n, cap))
        after = [mixed, sums]
        for i, k in enumerate(members):
            d_column[k] = sums[i]
    d_normed = z_reduce(d_column, n)

    grad_down = over_rows(active, grads_in)
    grad_gate = over_rows(d_gate, received)
    grad_up = over_rows(d_up, received)

    outcome = (hidden_wide + mixed).astype(BF)
    d_outcome = lax.dot_general(
        d_logits[0, 0, 0], own_head, (((0,), (0,)), ((), ())), precision=EXACT
    ) + grad_later.astype(F32)
    d_scaled = d_normed * own_gain[None, :]
    products = jnp.sum(d_scaled * hidden_wide, axis=1)
    slope = products
    for j in range(1, n):
        slope = slope + send_y(products, j)
    slope = slope[:, None] / model_width
    d_hidden = inv_rms * d_scaled - hidden_wide * (inv_rms * inv_rms * inv_rms) * slope
    grad_input = (d_outcome + d_hidden).astype(BF)
    return token_loss, outcome, grad_input, grad_gate, grad_up, grad_down


def solution(mesh):
    in_specs = (
        P("ep", "tp"),
        P("tp"),
        P("ep", None),
        P("ep", None),
        P("ep"),
        P("ep", "tp"),
        P("tp", None),
        P(("ep", "tp"), None),
        P(("ep", "tp"), None),
        P(("ep", "tp"), None),
    )
    out_specs = (
        P("ep"),
        P("ep", "tp"),
        P("ep", "tp"),
        P(("ep", "tp"), None),
        P(("ep", "tp"), None),
        P(("ep", "tp"), None),
    )
    return jax.shard_map(shards, mesh=mesh, in_specs=in_specs, out_specs=out_specs, check_vma=False)
```

```python
import functools

import jax
import jax.numpy as jnp
from jax import lax
from jax.experimental import pallas as pl
from jax.experimental.pallas import tpu as pltpu
from jax.sharding import PartitionSpec as P

FF = 768

EPS = 1e-06
LOSS_SCALE = 64.0
BF = jnp.bfloat16
F32 = jnp.float32
EXACT = lax.Precision.HIGHEST
VMEM_BYTES = 24 * 1024 * 1024
LANES = 128


def ring_sizes(dev_count):
    chips = dev_count // 2
    across = 1
    while across * across * 4 <= chips:
        across *= 2
    return across, chips // across


def send(value, target):
    dev_count, tp = lax.axis_size("ep"), lax.axis_size("tp")
    pairs = []
    for i in range(dev_count):
        for j in range(tp):
            a, b = target(i, j)
            pairs.append((i * tp + j, a * tp + b))
    return lax.ppermute(value, ("ep", "tp"), pairs)


def send_z(value, k, across):
    return send(value, lambda i, j: (i ^ (2 * across * k), j))


def send_core(value):
    return send(value, lambda i, j: (i ^ 1, j))


def send_x(value, k):
    return send(value, lambda i, j: (i ^ (2 * k), j))


def send_y(value, k):
    return send(value, lambda i, j: (i, j ^ k))


def send_first(value, k):
    return send(value, lambda i, j: (i, j ^ k) if i % 2 else (i ^ (2 * k), j))


def send_last(value, k):
    return send(value, lambda i, j: (i ^ (2 * k), j) if i % 2 else (i, j ^ k))


def z_gather(value, depth, n):
    column = {0: value}
    bit = depth // 2
    while bit:
        for k in list(column):
            column[k ^ bit] = send_z(column[k], bit, n)
        bit //= 2
    return [column[k] for k in range(depth)]


def z_reduce(column, n):
    blocks = dict(enumerate(column))
    bit = 1
    while bit < len(column):
        for k in sorted(blocks, reverse=True):
            if k & bit:
                blocks[k ^ bit] = blocks[k ^ bit] + send_z(blocks.pop(k).astype(BF), bit, n).astype(F32)
        bit *= 2
    return blocks[0]


def xor_blocks(value, axis, index):
    size = value.shape[axis]
    bit = 1
    while bit < size:
        shape = value.shape
        split = shape[:axis] + (size // (2 * bit), 2, bit) + shape[axis + 1 :]
        pairs = value.reshape(split)
        turned = jnp.flip(pairs, axis + 1)
        value = jnp.where((index & bit) > 0, turned, pairs).reshape(shape)
        bit *= 2
    return value


def params():
    return pltpu.CompilerParams(vmem_limit_bytes=VMEM_BYTES)


def whole_spec(shape):
    return pl.BlockSpec(shape, lambda *_: (0,) * len(shape))


def selector(pos_ref, h, z, cap, experts, tokens):
    slots = lax.broadcasted_iota(jnp.int32, (cap, tokens), 0).astype(F32)
    parts = [
        jnp.where(pos_ref[h, z, e : e + 1, :] == slots, 1.0, 0.0).astype(F32) for e in range(experts)
    ]
    return jnp.concatenate(parts, axis=0).astype(BF)


def pick_rows(units, after, pos, start, cap, joined=False):
    n, _, experts, tokens = pos.shape
    stacked = not isinstance(units[0], (list, tuple))
    group = units[0].shape[0] if stacked else len(units)
    flat = list(units) if stacked else [unit for at_z in units for unit in at_z]
    width = flat[0].shape[-1]

    def body(pos_ref, *refs):
        ins, outs = refs[: len(flat)], refs[len(flat) + len(after) :]
        for z in range(group):
            for h in range(n):
                chosen = selector(pos_ref, h, start + z, cap, experts, tokens)
                unit = ins[h][z] if stacked else ins[z * n + h][...]
                rows = jnp.dot(chosen, unit, preferred_element_type=F32).astype(BF)
                for e in range(experts):
                    part = rows[e * cap : (e + 1) * cap]
                    if joined:
                        outs[e // 2][e % 2, h, z] = part
                    else:
                        outs[e][h, z] = part

    vmem = pl.BlockSpec(memory_space=pltpu.VMEM)
    return pl.pallas_call(
        body,
        in_specs=[vmem] * (1 + len(flat)) + [pl.BlockSpec(memory_space=pl.ANY)] * len(after),
        out_specs=[vmem] * (n if joined else experts),
        out_shape=[jax.ShapeDtypeStruct((2, n, group, cap, width), BF)] * n
        if joined
        else [jax.ShapeDtypeStruct((n, group, cap, width), BF)] * experts,
        compiler_params=params(),
        cost_estimate=pl.CostEstimate(
            flops=2 * group * n * experts * cap * tokens * width,
            bytes_accessed=2 * group * n * width * (tokens + experts * cap),
            transcendentals=0,
        ),
        name="pick_rows",
    )(pos, *flat, *after)


def spread_rows(sources, after, pos, start, group, cap, width):
    n, _, experts, tokens = pos.shape

    def body(*refs):
        pos_ref, ins, outs = refs[0], refs[1 : 1 + experts], refs[-n:]
        for h in range(n):
            chosen = selector(pos_ref, h, 0, cap, experts, tokens)
            rows = jnp.concatenate(
                [ref[(0,) * len(prefix) + (h, 0)] for ref, (_, prefix) in zip(ins, sources)], axis=0
            )
            dense = lax.dot_general(chosen, rows, (((0,), (0,)), ((), ())), preferred_element_type=F32)
            outs[h][0] = dense.astype(BF)

    def spec(prefix):
        return pl.BlockSpec((1,) * len(prefix) + (n, 1, cap, width), lambda z: prefix + (0, z, 0, 0))

    return pl.pallas_call(
        body,
        grid=(group,),
        in_specs=[pl.BlockSpec((n, 1, experts, tokens), lambda z: (0, z + start, 0, 0))]
        + [spec(prefix) for _, prefix in sources]
        + [pl.BlockSpec(memory_space=pl.ANY)] * len(after),
        out_specs=[pl.BlockSpec((1, tokens, width), lambda z: (z, 0, 0))] * n,
        out_shape=[jax.ShapeDtypeStruct((group, tokens, width), BF)] * n,
        compiler_params=params(),
        cost_estimate=pl.CostEstimate(
            flops=2 * group * n * experts * cap * tokens * width,
            bytes_accessed=2 * group * n * width * (tokens + experts * cap),
            transcendentals=0,
        ),
        name="spread_rows",
    )(pos, *[array for array, _ in sources], *after)


def assemble(place, pieces, groups, finish, extra, extra_specs, after, model_width, name):
    n = len(pieces[0][0])
    _, _, cap, width = pieces[0][0][0].shape
    depth = sum(len(g) for g in groups)
    count = len(groups) * 2 * n

    def body(place_ref, *refs):
        ins, more, out_ref = refs[:count], refs[count : count + len(extra)], refs[-1]
        z = pl.program_id(0)
        core, col = place_ref[0], place_ref[1]

        def fill(g):
            for cr in range(2):
                kind = core ^ cr
                for f in range(n):
                    ref = ins[(g * 2 + cr) * n + f]
                    for h in range(n):
                        x = jnp.where(kind == 0, h, f)
                        y = jnp.where(kind == 0, f, h) ^ col
                        lanes = pl.ds(pl.multiple_of(y * width, LANES), width)
                        out_ref[0, cr * n + x, :, lanes] = ref[h, 0]

        for g, members in enumerate(groups):
            if len(groups) == 1:
                fill(g)
            else:
                pl.when(jnp.logical_and(z >= members[0], z <= members[-1]))(functools.partial(fill, g))
        finish(out_ref, *more)

    def piece_spec(members):
        first, last = members[0], members[-1]
        return pl.BlockSpec(
            (n, 1, cap, width), lambda z, *_: (0, jnp.clip(z, first, last) - first, 0, 0)
        )

    in_specs = [piece_spec(members) for members in groups for _ in range(2 * n)]
    flat = [piece for group in pieces for side in group for piece in side]
    return pl.pallas_call(
        body,
        grid_spec=pltpu.PrefetchScalarGridSpec(
            num_scalar_prefetch=1,
            grid=(depth,),
            in_specs=in_specs + extra_specs + [pl.BlockSpec(memory_space=pl.ANY)] * len(after),
            out_specs=pl.BlockSpec((1, 2 * n, cap, model_width), lambda z, *_: (z, 0, 0, 0)),
        ),
        out_shape=jax.ShapeDtypeStruct((depth, 2 * n, cap, model_width), BF),
        compiler_params=params(),
        cost_estimate=pl.CostEstimate(
            flops=10 * depth * 2 * n * cap * model_width,
            bytes_accessed=4 * depth * 2 * n * cap * model_width,
            transcendentals=0,
        ),
        name=name,
    )(place, *flat, *extra, *after)


def column_product(place, terms, scale, after, groups, depth, n, cap, width, name):
    count = len(terms)
    units = terms[0][0].shape[1]

    def where_to(y, b, place_ref):
        cr, x = b // n, b % n
        kind = place_ref[0] ^ cr
        y_rel = y ^ place_ref[1]
        return cr, jnp.where(kind == 0, y_rel, x), jnp.where(kind == 0, x, y_rel)

    def body(place_ref, *refs):
        total = None
        for i in range(count):
            left = refs[2 * i][...].reshape(depth * cap, units)
            term = jnp.dot(left, refs[2 * i + 1][...], preferred_element_type=F32)
            total = term if total is None else total + term
        rest = refs[2 * count :]
        rows = total.reshape(depth, cap, width)
        if scale is not None:
            rows = jnp.stack(
                [
                    rows[z] * row_weight(own_selector(rest[0][z, 0], cap), rest[1][z, 0])
                    for z in range(depth)
                ]
            )
            rest = rest[2:]
        rows = rows.astype(BF)
        rest = rest[len(after) :]
        for ref, members in zip(rest, groups):
            ref[0, 0, 0] = rows[members[0] : members[-1] + 1]

    left_spec = pl.BlockSpec((depth, 1, cap, units), lambda y, b, *_: (0, b, 0, 0))
    in_specs, args = [], []
    for left, right in terms:
        in_specs += [left_spec, pl.BlockSpec((units, width), lambda y, b, *_: (0, y))]
        args += [left.reshape(depth, 2 * n, cap, units), right]
    if scale is not None:
        in_specs += [
            pl.BlockSpec((depth, 1) + array.shape[2:], lambda y, b, *_: (0, b, 0, 0)) for array in scale
        ]
        args += scale
    in_specs += [pl.BlockSpec(memory_space=pl.ANY)] * len(after)
    args += after
    return pl.pallas_call(
        body,
        grid_spec=pltpu.PrefetchScalarGridSpec(
            num_scalar_prefetch=1,
            grid=(n, 2 * n),
            in_specs=in_specs,
            out_specs=[
                pl.BlockSpec(
                    (1, 1, 1, len(members), cap, width),
                    lambda y, b, place_ref: where_to(y, b, place_ref) + (0, 0, 0),
                )
                for members in groups
            ],
        ),
        out_shape=[
            jax.ShapeDtypeStruct((2, n, n, len(members), cap, width), BF) for members in groups
        ],
        compiler_params=params(),
        cost_estimate=pl.CostEstimate(
            flops=2 * count * depth * 2 * n * cap * units * width * n,
            bytes_accessed=2 * count * (units * width * n + depth * 2 * n * cap * units)
            + 2 * depth * 2 * n * cap * width * n,
            transcendentals=0,
        ),
        name=name,
    )(place, *args)


def own_selector(pos, cap):
    slots = lax.broadcasted_iota(jnp.int32, (cap, pos.shape[1]), 0).astype(F32)
    return jnp.where(pos == slots, 1.0, 0.0).astype(BF)


def wide_selector(pos_ref, blocks, cap):
    tokens = pos_ref.shape[-1]
    slots = lax.broadcasted_iota(jnp.int32, (blocks * cap, tokens), 0).astype(F32)
    parts = []
    for b in range(blocks):
        pos = pos_ref[0, b]
        parts.append(jnp.where(jnp.where(pos < 0, pos, pos + b * cap) == slots, 1.0, 0.0))
    return jnp.concatenate(parts, axis=1).astype(BF)


def row_weight(chosen, parts):
    picked = lax.dot_general(chosen, parts, (((1,), (1,)), ((), ())), preferred_element_type=F32)
    return picked[:, 0:1] + picked[:, 1:2] + picked[:, 2:3]


def row_sums(active, down_head, pos_own, weight_own, after, labels, depth, n, cap):
    units = active.shape[1]
    tokens = pos_own.shape[-1]

    def body(active_ref, head_ref, pos_ref, weight_ref, *rest):
        out_ref = rest[-1]
        chosen = wide_selector(pos_ref, 2 * n, cap)
        rows = active_ref[0].reshape(2 * n * cap, units)
        sums = lax.dot_general(head_ref[...], rows, (((1,), (1,)), ((), ())), preferred_element_type=F32)
        high = sums.astype(BF)
        low = (sums - high.astype(F32)).astype(BF)
        dense = jnp.dot(high, chosen, preferred_element_type=F32) + jnp.dot(
            low, chosen, preferred_element_type=F32
        )
        for b in range(2 * n):
            own = dense[:, b * tokens : (b + 1) * tokens]
            out_ref[0, b] = (own[0:labels] + own[8 : 8 + labels]) * weight_ref[0, b]

    return pl.pallas_call(
        body,
        grid=(depth,),
        in_specs=[
            pl.BlockSpec((1, 2 * n, cap, units), lambda z: (z, 0, 0, 0)),
            whole_spec(down_head.shape),
            pl.BlockSpec((1, 2 * n, 1, tokens), lambda z: (z, 0, 0, 0)),
            pl.BlockSpec((1, 2 * n, 1, tokens), lambda z: (z, 0, 0, 0)),
        ]
        + [pl.BlockSpec(memory_space=pl.ANY)] * len(after),
        out_specs=pl.BlockSpec((1, 2 * n, labels, tokens), lambda z: (z, 0, 0, 0)),
        out_shape=jax.ShapeDtypeStruct((depth, 2 * n, labels, tokens), F32),
        compiler_params=params(),
        cost_estimate=pl.CostEstimate(
            flops=2 * depth * 2 * n * cap * units * 16,
            bytes_accessed=2 * depth * 2 * n * cap * units,
            transcendentals=0,
        ),
        name="row_sums",
    )(active.reshape(depth, 2 * n, cap, units), down_head, pos_own, weight_own, *after)


def route_rows(units, after, pos, start, cap, joined=False):
    rows = pick_rows(units, after, pos, start, cap, joined)
    n = pos.shape[0]
    here, other = [], []
    for f in range(n):
        if joined:
            both = rows[f] if f == 0 else send_last(rows[f], f)
            same, cross = both[0], both[1]
        else:
            same, cross = rows[2 * f], rows[2 * f + 1]
            if f > 0:
                cross = send_last(cross, f)
                same = send_last(same, f)
        here.append(same)
        other.append(send_core(cross))
    return [here, other], rows


def gather_by_column(column, after, pos, groups, n, cap):
    units = [[value] + [send_first(value, k) for k in range(1, n)] for value in column]
    routed = [
        route_rows([units[k] for k in members], more, pos, members[0], cap)
        for members, more in zip(groups, after)
    ]
    return [pieces for pieces, _ in routed], routed[0][1]


def pick_at_once(column, pos, n, cap):
    column = jnp.stack(column)
    units = [column] + [send_first(column, k) for k in range(1, n)]
    pieces, rows = route_rows(units, [], pos, 0, cap, True)
    return [pieces], rows


def return_sources(rows, crossed, n):
    sources = [(rows, (0, 0)), (crossed, (0,))]
    for f in range(1, n):
        sources += [(send_last(rows[0, f], f), ()), (send_last(crossed[f], f), ())]
    return sources


def spread_back(rows, crossed, after, pos, start, n, cap):
    group, _, width = rows.shape[3:]
    return spread_rows(return_sources(rows, crossed, n), after, pos, start, group, cap, width)


def first_sum(dense):
    total = dense[0].astype(F32)
    for h in range(1, len(dense)):
        total = total + send_first(dense[h], h).astype(F32)
    return total


def sum_all(value, after, across, depth):
    value = value + send_core(value)
    step = 1
    while step < depth:
        value = value + send_z(value, step, across)
        step *= 2
    value = lax.optimization_barrier([value] + after)[0]
    step = 1
    while step < across:
        value = value + send_x(value, step)
        step *= 2
    step = 1
    while step < lax.axis_size("tp"):
        value = value + send_y(value, step)
        step *= 2
    return value


def split_bf(value, parts):
    pieces = []
    for _ in range(parts):
        piece = value.astype(BF)
        pieces.append(piece)
        value = value - piece.astype(F32)
    return pieces


def shards(
    hidden_in,
    norm_gain,
    expert_ids,
    routing_weight,
    labels,
    grad_later,
    head_weight,
    gate_weight,
    up_weight,
    down_weight,
):
    dev_count = lax.axis_size("ep")
    n = lax.axis_size("tp")
    row, col = lax.axis_index("ep"), lax.axis_index("tp")
    core = row & 1
    across, depth = ring_sizes(dev_count)
    if across != n:
        raise ValueError("x and y differ")
    tok_count, width = hidden_in.shape
    top_count = expert_ids.shape[1]
    model_width = gate_weight.shape[1]
    unit_rows = gate_weight.shape[0]
    local_count = unit_rows * n // FF
    expert_count = local_count * dev_count
    capacity = tok_count * top_count * 3 // (2 * expert_count)
    cap = -(-capacity // 16) * 16
    row_count = dev_count * cap
    label_count = head_weight.shape[1]
    place = jnp.stack([core, col]).astype(jnp.int32)
    two = [tuple(range(depth // 2)), tuple(range(depth // 2, depth))]
    one = [tuple(range(depth))]

    def expert_of(ep_index, tp_index):
        return ep_index * local_count + tp_index * unit_rows // FF

    hidden_column = z_gather(hidden_in, depth, n)

    spare = -(2 * top_count + 1) % 8
    meta = jnp.concatenate(
        [
            expert_ids.T.astype(F32),
            routing_weight.T,
            labels.astype(F32)[None, :],
            jnp.zeros((spare, tok_count), F32),
        ]
    )
    meta = jnp.stack(z_gather(meta, depth, n))
    meta = jnp.stack([meta] + [send_x(meta, k) for k in range(1, n)], axis=1)
    meta = jnp.stack([meta, send_core(meta)], axis=1)

    hidden_wide = hidden_in.astype(F32)
    own_squares = jnp.sum(hidden_wide * hidden_wide, axis=1)
    feature_rows = jnp.concatenate(
        [
            norm_gain[None, :],
            head_weight.astype(F32).T,
            jnp.pad(own_squares[None, :], ((0, 0), (0, width - tok_count))),
            jnp.zeros((-(2 + label_count) % 8, width), F32),
        ]
    )
    own_gain, own_head = feature_rows[0], feature_rows[1 : 1 + label_count]
    all_features = jnp.stack([feature_rows] + [send_y(feature_rows, j) for j in range(1, n)], axis=1)
    squares = jnp.sum(all_features[1 + label_count, :, :tok_count], axis=0)
    inv_rms = lax.rsqrt(squares / model_width + EPS)[:, None]
    all_features = xor_blocks(all_features, 1, col).reshape(feature_rows.shape[0], model_width)

    spot = jnp.arange(tok_count, dtype=jnp.int32)
    earlier = (spot[:, None] < spot[None, :]).astype(BF)

    def positions(ids, experts):
        member = jnp.stack([jnp.sum((ids == e.astype(F32)).astype(F32), axis=-2) for e in experts], axis=-2)
        before = lax.dot_general(
            member.astype(BF), earlier, (((member.ndim - 1,), (0,)), ((), ())), preferred_element_type=F32
        )
        return jnp.where(member > 0, before, -1.0)

    ids = meta[..., :top_count, :]
    near = [expert_of(row, col), expert_of(row ^ 1, col)]
    for f in range(1, n):
        far_row = jnp.where(core == 0, row, row ^ (2 * f))
        far_col = jnp.where(core == 0, col ^ f, col)
        near += [expert_of(far_row, far_col), expert_of(far_row ^ 1, far_col)]
    unit_ids = jnp.stack([jnp.where(core == 0, ids[:, 0, h], ids[:, 0, 0]) for h in range(n)])
    pos = positions(unit_ids, near)
    blocks = ids.reshape(depth, 2 * n, top_count, tok_count)
    pos_own = positions(blocks, [expert_of(row, col)])
    named_own = (blocks == expert_of(row, col).astype(F32)).astype(F32)
    weights = meta[..., top_count : 2 * top_count, :].reshape(blocks.shape)
    weight_own = jnp.sum(named_own * weights, axis=-2, keepdims=True)
    blank = jnp.zeros((depth, 2 * n, 13, tok_count), BF)
    weight_parts = jnp.concatenate(split_bf(weight_own, 3) + [blank], axis=2)
    label_all = meta[..., 2 * top_count, :]

    head_pair = jnp.concatenate(
        [all_features[1 : 1 + label_count], jnp.zeros((8 - label_count, model_width), F32)]
    )
    head_pair = jnp.concatenate([head_pair, head_pair]).astype(BF)
    down_head = lax.dot_general(
        head_pair, down_weight, (((1,), (1,)), ((), ())), preferred_element_type=F32
    )
    high = down_head.astype(BF)
    which = lax.broadcasted_iota(jnp.int32, down_head.shape, 0)
    down_head = jnp.where(which < 8, high, (down_head - high.astype(F32)).astype(BF))

    later_in = lax.optimization_barrier([grad_later, hidden_column[depth // 2]])[0]
    later_column = z_gather(later_in, depth, n)
    pieces, _ = gather_by_column(hidden_column, [[], later_column[depth // 2 : depth // 2 + 1]], pos, two, n, cap)

    def normed(out_ref, features_ref):
        for b in range(2 * n):
            value = out_ref[0, b].astype(F32)
            rms = lax.rsqrt(jnp.sum(value * value, axis=1, keepdims=True) / model_width + EPS)
            out_ref[0, b] = (value * rms * features_ref[0:1, :]).astype(BF)

    received = assemble(
        place,
        pieces,
        two,
        normed,
        [all_features],
        [whole_spec(all_features.shape)],
        [],
        model_width,
        "normed_rows",
    ).reshape(row_count, model_width)
    later, picked_later = pick_at_once(later_column, pos, n, cap)

    def against(left, right):
        return lax.dot_general(left, right, (((1,), (1,)), ((), ())), preferred_element_type=F32)

    def over_rows(left, right):
        return lax.dot_general(left, right, (((0,), (0,)), ((), ())), preferred_element_type=F32).astype(BF)

    gate_pre = against(received, gate_weight)
    up_pre = against(received, up_weight)
    sigma = jax.nn.sigmoid(gate_pre)
    active = (gate_pre * sigma * up_pre).astype(BF)

    logits = row_sums(active, down_head, pos_own, weight_own, list(picked_later[:1]), label_count, depth, n, cap)
    out_rows = column_product(
        place, [(active, down_weight)], [pos_own, weight_parts], list(picked_later[:1]), one, depth, n, cap, width, "out_rows"
    )[0]
    crossed = send_core(out_rows[1])
    out_dense = spread_back(out_rows, crossed, [], pos, 0, n, cap)
    out_column = first_sum(out_dense)
    own_logits = lax.dot_general(
        own_head.astype(BF), hidden_in, (((1,), (1,)), ((), ())), preferred_element_type=F32
    )

    def turn(value):
        value = value.reshape((depth, 2, n) + value.shape[-2:])
        value = xor_blocks(value, 0, row // (2 * across))
        value = xor_blocks(value, 1, core)
        return xor_blocks(value, 2, (row // 2) & (across - 1))

    block = jnp.arange(depth * 2 * n).reshape(depth, 2 * n)
    logits = logits + jnp.where((block == 0)[..., None, None], own_logits, 0.0)
    logits = turn(sum_all(turn(logits), later[0][0] + later[0][1], across, depth))
    classes = (label_all[..., None, :] == jnp.arange(label_count, dtype=F32)[:, None]).astype(F32)
    powers = jnp.exp(logits)
    totals = jnp.sum(powers, axis=-2, keepdims=True)
    d_logits = (powers / totals - classes) * LOSS_SCALE
    token_loss = jnp.log(totals[0, 0, 0, 0]) - jnp.sum(logits[0, 0, 0] * classes[0, 0, 0], axis=0)

    d_parts = jnp.concatenate(
        split_bf(d_logits.reshape(depth, 2 * n, label_count, tok_count), 2)
        + [weight_parts[:, :, : 16 - 2 * label_count]],
        axis=2,
    )

    keys = jnp.concatenate([all_features[1 : 1 + label_count]] * 2)
    keys = jnp.concatenate([keys, jnp.zeros((16 - 2 * label_count, model_width), F32)]).astype(BF)

    def gradient_rows(out_ref, keys_ref, pos_ref, parts_ref):
        chosen = wide_selector(pos_ref, 2 * n, cap)
        parts = jnp.concatenate([parts_ref[0, b] for b in range(2 * n)], axis=1)
        picked = lax.dot_general(chosen, parts, (((1,), (1,)), ((), ())), preferred_element_type=F32)
        first = 2 * label_count
        weight = picked[:, first : first + 1] + picked[:, first + 1 : first + 2] + picked[:, first + 2 : first + 3]
        head_term = jnp.dot(picked.astype(BF), keys_ref[...], preferred_element_type=F32)
        for b in range(2 * n):
            part = slice(b * cap, (b + 1) * cap)
            value = head_term[part] + out_ref[0, b].astype(F32)
            out_ref[0, b] = (value.astype(BF).astype(F32) * weight[part]).astype(BF)

    grads_in = assemble(
        place,
        later,
        one,
        gradient_rows,
        [keys, pos_own, d_parts],
        [
            whole_spec(keys.shape),
            pl.BlockSpec((1, 2 * n, 1, tok_count), lambda z, *_: (z, 0, 0, 0)),
            pl.BlockSpec((1, 2 * n, 16, tok_count), lambda z, *_: (z, 0, 0, 0)),
        ],
        [crossed],
        model_width,
        "gradient_rows",
    ).reshape(row_count, model_width)

    d_active = against(grads_in, down_weight)
    d_gate = (d_active * up_pre * sigma * (1.0 + gate_pre * (1.0 - sigma))).astype(BF)
    d_up = (d_active * gate_pre * sigma).astype(BF)

    d_rows = column_product(
        place, [(d_gate, gate_weight), (d_up, up_weight)], None, list(out_dense[:1]), two, depth, n, cap, width, "d_rows"
    )
    mixed = z_reduce(out_column, n)
    d_column = [None] * depth
    after = []
    for rows, members in reversed(list(zip(d_rows, two))):
        sums = first_sum(spread_back(rows, send_core(rows[1]), after, pos, members[0], n, cap))
        after = [mixed, sums]
        for i, k in enumerate(members):
            d_column[k] = sums[i]
    d_normed = z_reduce(d_column, n)

    grad_down = over_rows(active, grads_in)
    grad_gate = over_rows(d_gate, received)
    grad_up = over_rows(d_up, received)

    outcome = (hidden_wide + mixed).astype(BF)
    d_outcome = lax.dot_general(
        d_logits[0, 0, 0], own_head, (((0,), (0,)), ((), ())), precision=EXACT
    ) + grad_later.astype(F32)
    d_scaled = d_normed * own_gain[None, :]
    products = jnp.sum(d_scaled * hidden_wide, axis=1)
    slope = products
    for j in range(1, n):
        slope = slope + send_y(products, j)
    slope = slope[:, None] / model_width
    d_hidden = inv_rms * d_scaled - hidden_wide * (inv_rms * inv_rms * inv_rms) * slope
    grad_input = (d_outcome + d_hidden).astype(BF)
    return token_loss, outcome, grad_input, grad_gate, grad_up, grad_down


def solution(mesh):
    in_specs = (
        P("ep", "tp"),
        P("tp"),
        P("ep", None),
        P("ep", None),
        P("ep"),
        P("ep", "tp"),
        P("tp", None),
        P(("ep", "tp"), None),
        P(("ep", "tp"), None),
        P(("ep", "tp"), None),
    )
    out_specs = (
        P("ep"),
        P("ep", "tp"),
        P("ep", "tp"),
        P(("ep", "tp"), None),
        P(("ep", "tp"), None),
        P(("ep", "tp"), None),
    )
    return jax.shard_map(shards, mesh=mesh, in_specs=in_specs, out_specs=out_specs, check_vma=False)
```

```python
import functools

import jax
import jax.numpy as jnp
from jax import lax
from jax.experimental import pallas as pl
from jax.experimental.pallas import tpu as pltpu
from jax.sharding import PartitionSpec as P

FF = 768

EPS = 1e-06
LOSS_SCALE = 64.0
BF = jnp.bfloat16
F32 = jnp.float32
EXACT = lax.Precision.HIGHEST
VMEM_BYTES = 24 * 1024 * 1024
LANES = 128


def ring_sizes(dev_count):
    chips = dev_count // 2
    across = 1
    while across * across * 4 <= chips:
        across *= 2
    return across, chips // across


def send(value, target):
    dev_count, tp = lax.axis_size("ep"), lax.axis_size("tp")
    pairs = []
    for i in range(dev_count):
        for j in range(tp):
            a, b = target(i, j)
            pairs.append((i * tp + j, a * tp + b))
    return lax.ppermute(value, ("ep", "tp"), pairs)


def send_z(value, k, across):
    return send(value, lambda i, j: (i ^ (2 * across * k), j))


def send_core(value):
    return send(value, lambda i, j: (i ^ 1, j))


def send_x(value, k):
    return send(value, lambda i, j: (i ^ (2 * k), j))


def send_y(value, k):
    return send(value, lambda i, j: (i, j ^ k))


def send_first(value, k):
    return send(value, lambda i, j: (i, j ^ k) if i % 2 else (i ^ (2 * k), j))


def send_last(value, k):
    return send(value, lambda i, j: (i ^ (2 * k), j) if i % 2 else (i, j ^ k))


def z_gather(value, depth, n):
    column = {0: value}
    bit = depth // 2
    while bit:
        for k in list(column):
            column[k ^ bit] = send_z(column[k], bit, n)
        bit //= 2
    return [column[k] for k in range(depth)]


def z_reduce(column, n):
    blocks = dict(enumerate(column))
    bit = 1
    while bit < len(column):
        for k in sorted(blocks, reverse=True):
            if k & bit:
                blocks[k ^ bit] = blocks[k ^ bit] + send_z(blocks.pop(k).astype(BF), bit, n).astype(F32)
        bit *= 2
    return blocks[0]


def xor_blocks(value, axis, index):
    size = value.shape[axis]
    bit = 1
    while bit < size:
        shape = value.shape
        split = shape[:axis] + (size // (2 * bit), 2, bit) + shape[axis + 1 :]
        pairs = value.reshape(split)
        turned = jnp.flip(pairs, axis + 1)
        value = jnp.where((index & bit) > 0, turned, pairs).reshape(shape)
        bit *= 2
    return value


def params():
    return pltpu.CompilerParams(vmem_limit_bytes=VMEM_BYTES)


def whole_spec(shape):
    return pl.BlockSpec(shape, lambda *_: (0,) * len(shape))


def selector(pos_ref, h, z, cap, experts, tokens):
    slots = lax.broadcasted_iota(jnp.int32, (cap, tokens), 0).astype(F32)
    parts = [
        jnp.where(pos_ref[h, z, e : e + 1, :] == slots, 1.0, 0.0).astype(F32) for e in range(experts)
    ]
    return jnp.concatenate(parts, axis=0).astype(BF)


def pick_rows(units, after, pos, start, cap, joined=False):
    n, _, experts, tokens = pos.shape
    stacked = not isinstance(units[0], (list, tuple))
    group = units[0].shape[0] if stacked else len(units)
    flat = list(units) if stacked else [unit for at_z in units for unit in at_z]
    width = flat[0].shape[-1]

    def body(pos_ref, *refs):
        ins, outs = refs[: len(flat)], refs[len(flat) + len(after) :]
        for z in range(group):
            for h in range(n):
                chosen = selector(pos_ref, h, start + z, cap, experts, tokens)
                unit = ins[h][z] if stacked else ins[z * n + h][...]
                rows = jnp.dot(chosen, unit, preferred_element_type=F32).astype(BF)
                for e in range(experts):
                    part = rows[e * cap : (e + 1) * cap]
                    if joined:
                        outs[e // 2][e % 2, h, z] = part
                    else:
                        outs[e][h, z] = part

    vmem = pl.BlockSpec(memory_space=pltpu.VMEM)
    return pl.pallas_call(
        body,
        in_specs=[vmem] * (1 + len(flat)) + [pl.BlockSpec(memory_space=pl.ANY)] * len(after),
        out_specs=[vmem] * (n if joined else experts),
        out_shape=[jax.ShapeDtypeStruct((2, n, group, cap, width), BF)] * n
        if joined
        else [jax.ShapeDtypeStruct((n, group, cap, width), BF)] * experts,
        compiler_params=params(),
        cost_estimate=pl.CostEstimate(
            flops=2 * group * n * experts * cap * tokens * width,
            bytes_accessed=2 * group * n * width * (tokens + experts * cap),
            transcendentals=0,
        ),
        name="pick_rows",
    )(pos, *flat, *after)


def spread_rows(sources, after, pos, start, group, cap, width):
    n, _, experts, tokens = pos.shape

    def body(*refs):
        pos_ref, ins, outs = refs[0], refs[1 : 1 + experts], refs[-n:]
        for h in range(n):
            chosen = selector(pos_ref, h, 0, cap, experts, tokens)
            rows = jnp.concatenate(
                [ref[(0,) * len(prefix) + (h, 0)] for ref, (_, prefix) in zip(ins, sources)], axis=0
            )
            dense = lax.dot_general(chosen, rows, (((0,), (0,)), ((), ())), preferred_element_type=F32)
            outs[h][0] = dense.astype(BF)

    def spec(prefix):
        return pl.BlockSpec((1,) * len(prefix) + (n, 1, cap, width), lambda z: prefix + (0, z, 0, 0))

    return pl.pallas_call(
        body,
        grid=(group,),
        in_specs=[pl.BlockSpec((n, 1, experts, tokens), lambda z: (0, z + start, 0, 0))]
        + [spec(prefix) for _, prefix in sources]
        + [pl.BlockSpec(memory_space=pl.ANY)] * len(after),
        out_specs=[pl.BlockSpec((1, tokens, width), lambda z: (z, 0, 0))] * n,
        out_shape=[jax.ShapeDtypeStruct((group, tokens, width), BF)] * n,
        compiler_params=params(),
        cost_estimate=pl.CostEstimate(
            flops=2 * group * n * experts * cap * tokens * width,
            bytes_accessed=2 * group * n * width * (tokens + experts * cap),
            transcendentals=0,
        ),
        name="spread_rows",
    )(pos, *[array for array, _ in sources], *after)


def assemble(place, pieces, groups, finish, extra, extra_specs, after, model_width, name):
    n = len(pieces[0][0])
    _, _, cap, width = pieces[0][0][0].shape
    depth = sum(len(g) for g in groups)
    count = len(groups) * 2 * n

    def body(place_ref, *refs):
        ins, more, out_ref = refs[:count], refs[count : count + len(extra)], refs[-1]
        z = pl.program_id(0)
        core, col = place_ref[0], place_ref[1]

        def fill(g):
            for cr in range(2):
                kind = core ^ cr
                for f in range(n):
                    ref = ins[(g * 2 + cr) * n + f]
                    for h in range(n):
                        x = jnp.where(kind == 0, h, f)
                        y = jnp.where(kind == 0, f, h) ^ col
                        lanes = pl.ds(pl.multiple_of(y * width, LANES), width)
                        out_ref[0, cr * n + x, :, lanes] = ref[h, 0]

        for g, members in enumerate(groups):
            if len(groups) == 1:
                fill(g)
            else:
                pl.when(jnp.logical_and(z >= members[0], z <= members[-1]))(functools.partial(fill, g))
        finish(out_ref, *more)

    def piece_spec(members):
        first, last = members[0], members[-1]
        return pl.BlockSpec(
            (n, 1, cap, width), lambda z, *_: (0, jnp.clip(z, first, last) - first, 0, 0)
        )

    in_specs = [piece_spec(members) for members in groups for _ in range(2 * n)]
    flat = [piece for group in pieces for side in group for piece in side]
    return pl.pallas_call(
        body,
        grid_spec=pltpu.PrefetchScalarGridSpec(
            num_scalar_prefetch=1,
            grid=(depth,),
            in_specs=in_specs + extra_specs + [pl.BlockSpec(memory_space=pl.ANY)] * len(after),
            out_specs=pl.BlockSpec((1, 2 * n, cap, model_width), lambda z, *_: (z, 0, 0, 0)),
        ),
        out_shape=jax.ShapeDtypeStruct((depth, 2 * n, cap, model_width), BF),
        compiler_params=params(),
        cost_estimate=pl.CostEstimate(
            flops=10 * depth * 2 * n * cap * model_width,
            bytes_accessed=4 * depth * 2 * n * cap * model_width,
            transcendentals=0,
        ),
        name=name,
    )(place, *flat, *extra, *after)


def column_product(place, terms, scale, after, groups, depth, n, cap, width, name):
    count = len(terms)
    units = terms[0][0].shape[1]

    def where_to(y, b, place_ref):
        cr, x = b // n, b % n
        kind = place_ref[0] ^ cr
        y_rel = y ^ place_ref[1]
        return cr, jnp.where(kind == 0, y_rel, x), jnp.where(kind == 0, x, y_rel)

    def body(place_ref, *refs):
        total = None
        for i in range(count):
            left = refs[2 * i][...].reshape(depth * cap, units)
            term = jnp.dot(left, refs[2 * i + 1][...], preferred_element_type=F32)
            total = term if total is None else total + term
        rest = refs[2 * count :]
        rows = total.reshape(depth, cap, width)
        if scale is not None:
            rows = jnp.stack(
                [
                    rows[z] * row_weight(own_selector(rest[0][z, 0], cap), rest[1][z, 0])
                    for z in range(depth)
                ]
            )
            rest = rest[2:]
        rows = rows.astype(BF)
        rest = rest[len(after) :]
        for ref, members in zip(rest, groups):
            ref[0, 0, 0] = rows[members[0] : members[-1] + 1]

    left_spec = pl.BlockSpec((depth, 1, cap, units), lambda y, b, *_: (0, b, 0, 0))
    in_specs, args = [], []
    for left, right in terms:
        in_specs += [left_spec, pl.BlockSpec((units, width), lambda y, b, *_: (0, y))]
        args += [left.reshape(depth, 2 * n, cap, units), right]
    if scale is not None:
        in_specs += [
            pl.BlockSpec((depth, 1) + array.shape[2:], lambda y, b, *_: (0, b, 0, 0)) for array in scale
        ]
        args += scale
    in_specs += [pl.BlockSpec(memory_space=pl.ANY)] * len(after)
    args += after
    return pl.pallas_call(
        body,
        grid_spec=pltpu.PrefetchScalarGridSpec(
            num_scalar_prefetch=1,
            grid=(n, 2 * n),
            in_specs=in_specs,
            out_specs=[
                pl.BlockSpec(
                    (1, 1, 1, len(members), cap, width),
                    lambda y, b, place_ref: where_to(y, b, place_ref) + (0, 0, 0),
                )
                for members in groups
            ],
        ),
        out_shape=[
            jax.ShapeDtypeStruct((2, n, n, len(members), cap, width), BF) for members in groups
        ],
        compiler_params=params(),
        cost_estimate=pl.CostEstimate(
            flops=2 * count * depth * 2 * n * cap * units * width * n,
            bytes_accessed=2 * count * (units * width * n + depth * 2 * n * cap * units)
            + 2 * depth * 2 * n * cap * width * n,
            transcendentals=0,
        ),
        name=name,
    )(place, *args)


def own_selector(pos, cap):
    slots = lax.broadcasted_iota(jnp.int32, (cap, pos.shape[1]), 0).astype(F32)
    return jnp.where(pos == slots, 1.0, 0.0).astype(BF)


def wide_selector(pos_ref, blocks, cap):
    tokens = pos_ref.shape[-1]
    slots = lax.broadcasted_iota(jnp.int32, (blocks * cap, tokens), 0).astype(F32)
    parts = []
    for b in range(blocks):
        pos = pos_ref[0, b]
        parts.append(jnp.where(jnp.where(pos < 0, pos, pos + b * cap) == slots, 1.0, 0.0))
    return jnp.concatenate(parts, axis=1).astype(BF)


def row_weight(chosen, parts):
    picked = lax.dot_general(chosen, parts, (((1,), (1,)), ((), ())), preferred_element_type=F32)
    return picked[:, 0:1] + picked[:, 1:2] + picked[:, 2:3]


def row_sums(active, down_head, pos_own, weight_own, after, labels, depth, n, cap):
    units = active.shape[1]
    tokens = pos_own.shape[-1]

    def body(active_ref, head_ref, pos_ref, weight_ref, *rest):
        out_ref = rest[-1]
        chosen = wide_selector(pos_ref, 2 * n, cap)
        rows = active_ref[0].reshape(2 * n * cap, units)
        sums = lax.dot_general(head_ref[...], rows, (((1,), (1,)), ((), ())), preferred_element_type=F32)
        high = sums.astype(BF)
        low = (sums - high.astype(F32)).astype(BF)
        dense = jnp.dot(high, chosen, preferred_element_type=F32) + jnp.dot(
            low, chosen, preferred_element_type=F32
        )
        for b in range(2 * n):
            own = dense[:, b * tokens : (b + 1) * tokens]
            out_ref[0, b] = (own[0:labels] + own[8 : 8 + labels]) * weight_ref[0, b]

    return pl.pallas_call(
        body,
        grid=(depth,),
        in_specs=[
            pl.BlockSpec((1, 2 * n, cap, units), lambda z: (z, 0, 0, 0)),
            whole_spec(down_head.shape),
            pl.BlockSpec((1, 2 * n, 1, tokens), lambda z: (z, 0, 0, 0)),
            pl.BlockSpec((1, 2 * n, 1, tokens), lambda z: (z, 0, 0, 0)),
        ]
        + [pl.BlockSpec(memory_space=pl.ANY)] * len(after),
        out_specs=pl.BlockSpec((1, 2 * n, labels, tokens), lambda z: (z, 0, 0, 0)),
        out_shape=jax.ShapeDtypeStruct((depth, 2 * n, labels, tokens), F32),
        compiler_params=params(),
        cost_estimate=pl.CostEstimate(
            flops=2 * depth * 2 * n * cap * units * 16,
            bytes_accessed=2 * depth * 2 * n * cap * units,
            transcendentals=0,
        ),
        name="row_sums",
    )(active.reshape(depth, 2 * n, cap, units), down_head, pos_own, weight_own, *after)


def route_rows(units, after, pos, start, cap, joined=False):
    rows = pick_rows(units, after, pos, start, cap, joined)
    n = pos.shape[0]
    here, other = [], []
    for f in range(n):
        if joined:
            both = rows[f] if f == 0 else send_last(rows[f], f)
            same, cross = both[0], both[1]
        else:
            same, cross = rows[2 * f], rows[2 * f + 1]
            if f > 0:
                cross = send_last(cross, f)
                same = send_last(same, f)
        here.append(same)
        other.append(send_core(cross))
    return [here, other], rows


def gather_by_column(column, after, pos, groups, n, cap):
    units = [[value] + [send_first(value, k) for k in range(1, n)] for value in column]
    routed = []
    for members, more in zip(groups, after):
        more = more + [rows[0] for _, rows in routed]
        routed.append(route_rows([units[k] for k in members], more, pos, members[0], cap))
    return [pieces for pieces, _ in routed], routed[0][1]


def pick_at_once(column, pos, n, cap):
    column = jnp.stack(column)
    units = [column] + [send_first(column, k) for k in range(1, n)]
    pieces, rows = route_rows(units, [], pos, 0, cap, True)
    return [pieces], rows


def return_sources(rows, crossed, n):
    sources = [(rows, (0, 0)), (crossed, (0,))]
    for f in range(1, n):
        sources += [(send_last(rows[0, f], f), ()), (send_last(crossed[f], f), ())]
    return sources


def spread_back(rows, crossed, after, pos, start, n, cap):
    group, _, width = rows.shape[3:]
    return spread_rows(return_sources(rows, crossed, n), after, pos, start, group, cap, width)


def first_sum(dense):
    total = dense[0].astype(F32)
    for h in range(1, len(dense)):
        total = total + send_first(dense[h], h).astype(F32)
    return total


def sum_all(value, after, across, depth):
    value = value + send_core(value)
    step = 1
    while step < depth:
        value = value + send_z(value, step, across)
        step *= 2
    value = lax.optimization_barrier([value] + after)[0]
    step = 1
    while step < across:
        value = value + send_x(value, step)
        step *= 2
    step = 1
    while step < lax.axis_size("tp"):
        value = value + send_y(value, step)
        step *= 2
    return value


def split_bf(value, parts):
    pieces = []
    for _ in range(parts):
        piece = value.astype(BF)
        pieces.append(piece)
        value = value - piece.astype(F32)
    return pieces


def shards(
    hidden_in,
    norm_gain,
    expert_ids,
    routing_weight,
    labels,
    grad_later,
    head_weight,
    gate_weight,
    up_weight,
    down_weight,
):
    dev_count = lax.axis_size("ep")
    n = lax.axis_size("tp")
    row, col = lax.axis_index("ep"), lax.axis_index("tp")
    core = row & 1
    across, depth = ring_sizes(dev_count)
    if across != n:
        raise ValueError("x and y differ")
    tok_count, width = hidden_in.shape
    top_count = expert_ids.shape[1]
    model_width = gate_weight.shape[1]
    unit_rows = gate_weight.shape[0]
    local_count = unit_rows * n // FF
    expert_count = local_count * dev_count
    capacity = tok_count * top_count * 3 // (2 * expert_count)
    cap = -(-capacity // 16) * 16
    row_count = dev_count * cap
    label_count = head_weight.shape[1]
    place = jnp.stack([core, col]).astype(jnp.int32)
    two = [tuple(range(depth // 2)), tuple(range(depth // 2, depth))]
    one = [tuple(range(depth))]

    def expert_of(ep_index, tp_index):
        return ep_index * local_count + tp_index * unit_rows // FF

    hidden_column = z_gather(hidden_in, depth, n)

    spare = -(2 * top_count + 1) % 8
    meta = jnp.concatenate(
        [
            expert_ids.T.astype(F32),
            routing_weight.T,
            labels.astype(F32)[None, :],
            jnp.zeros((spare, tok_count), F32),
        ]
    )
    meta = jnp.stack(z_gather(meta, depth, n))
    meta = jnp.stack([meta] + [send_x(meta, k) for k in range(1, n)], axis=1)
    meta = jnp.stack([meta, send_core(meta)], axis=1)

    hidden_wide = hidden_in.astype(F32)
    own_squares = jnp.sum(hidden_wide * hidden_wide, axis=1)
    feature_rows = jnp.concatenate(
        [
            norm_gain[None, :],
            head_weight.astype(F32).T,
            jnp.pad(own_squares[None, :], ((0, 0), (0, width - tok_count))),
            jnp.zeros((-(2 + label_count) % 8, width), F32),
        ]
    )
    own_gain, own_head = feature_rows[0], feature_rows[1 : 1 + label_count]
    all_features = jnp.stack([feature_rows] + [send_y(feature_rows, j) for j in range(1, n)], axis=1)
    squares = jnp.sum(all_features[1 + label_count, :, :tok_count], axis=0)
    inv_rms = lax.rsqrt(squares / model_width + EPS)[:, None]
    all_features = xor_blocks(all_features, 1, col).reshape(feature_rows.shape[0], model_width)

    spot = jnp.arange(tok_count, dtype=jnp.int32)
    earlier = (spot[:, None] < spot[None, :]).astype(BF)

    def positions(ids, experts):
        member = jnp.stack([jnp.sum((ids == e.astype(F32)).astype(F32), axis=-2) for e in experts], axis=-2)
        before = lax.dot_general(
            member.astype(BF), earlier, (((member.ndim - 1,), (0,)), ((), ())), preferred_element_type=F32
        )
        return jnp.where(member > 0, before, -1.0)

    ids = meta[..., :top_count, :]
    near = [expert_of(row, col), expert_of(row ^ 1, col)]
    for f in range(1, n):
        far_row = jnp.where(core == 0, row, row ^ (2 * f))
        far_col = jnp.where(core == 0, col ^ f, col)
        near += [expert_of(far_row, far_col), expert_of(far_row ^ 1, far_col)]
    unit_ids = jnp.stack([jnp.where(core == 0, ids[:, 0, h], ids[:, 0, 0]) for h in range(n)])
    pos = positions(unit_ids, near)
    blocks = ids.reshape(depth, 2 * n, top_count, tok_count)
    pos_own = positions(blocks, [expert_of(row, col)])
    named_own = (blocks == expert_of(row, col).astype(F32)).astype(F32)
    weights = meta[..., top_count : 2 * top_count, :].reshape(blocks.shape)
    weight_own = jnp.sum(named_own * weights, axis=-2, keepdims=True)
    blank = jnp.zeros((depth, 2 * n, 13, tok_count), BF)
    weight_parts = jnp.concatenate(split_bf(weight_own, 3) + [blank], axis=2)
    label_all = meta[..., 2 * top_count, :]

    head_pair = jnp.concatenate(
        [all_features[1 : 1 + label_count], jnp.zeros((8 - label_count, model_width), F32)]
    )
    head_pair = jnp.concatenate([head_pair, head_pair]).astype(BF)
    down_head = lax.dot_general(
        head_pair, down_weight, (((1,), (1,)), ((), ())), preferred_element_type=F32
    )
    high = down_head.astype(BF)
    which = lax.broadcasted_iota(jnp.int32, down_head.shape, 0)
    down_head = jnp.where(which < 8, high, (down_head - high.astype(F32)).astype(BF))

    later_in = lax.optimization_barrier([grad_later, hidden_column[depth // 2]])[0]
    later_column = z_gather(later_in, depth, n)
    pieces, _ = gather_by_column(hidden_column, [[down_head], later_column[depth // 2 : depth // 2 + 1]], pos, two, n, cap)

    def normed(out_ref, features_ref):
        for b in range(2 * n):
            value = out_ref[0, b].astype(F32)
            rms = lax.rsqrt(jnp.sum(value * value, axis=1, keepdims=True) / model_width + EPS)
            out_ref[0, b] = (value * rms * features_ref[0:1, :]).astype(BF)

    received = assemble(
        place,
        pieces,
        two,
        normed,
        [all_features],
        [whole_spec(all_features.shape)],
        [],
        model_width,
        "normed_rows",
    ).reshape(row_count, model_width)
    later, picked_later = pick_at_once(later_column, pos, n, cap)

    def against(left, right):
        return lax.dot_general(left, right, (((1,), (1,)), ((), ())), preferred_element_type=F32)

    def over_rows(left, right):
        return lax.dot_general(left, right, (((0,), (0,)), ((), ())), preferred_element_type=F32).astype(BF)

    gate_pre = against(received, gate_weight)
    up_pre = against(received, up_weight)
    sigma = jax.nn.sigmoid(gate_pre)
    active = (gate_pre * sigma * up_pre).astype(BF)

    logits = row_sums(active, down_head, pos_own, weight_own, list(picked_later[:1]), label_count, depth, n, cap)
    out_rows = column_product(
        place, [(active, down_weight)], [pos_own, weight_parts], list(picked_later[:1]), one, depth, n, cap, width, "out_rows"
    )[0]
    crossed = send_core(out_rows[1])
    out_dense = spread_back(out_rows, crossed, [], pos, 0, n, cap)
    out_column = first_sum(out_dense)
    own_logits = lax.dot_general(
        own_head.astype(BF), hidden_in, (((1,), (1,)), ((), ())), preferred_element_type=F32
    )

    def turn(value):
        value = value.reshape((depth, 2, n) + value.shape[-2:])
        value = xor_blocks(value, 0, row // (2 * across))
        value = xor_blocks(value, 1, core)
        return xor_blocks(value, 2, (row // 2) & (across - 1))

    block = jnp.arange(depth * 2 * n).reshape(depth, 2 * n)
    logits = logits + jnp.where((block == 0)[..., None, None], own_logits, 0.0)
    logits = turn(sum_all(turn(logits), later[0][0] + later[0][1], across, depth))
    classes = (label_all[..., None, :] == jnp.arange(label_count, dtype=F32)[:, None]).astype(F32)
    powers = jnp.exp(logits)
    totals = jnp.sum(powers, axis=-2, keepdims=True)
    d_logits = (powers / totals - classes) * LOSS_SCALE
    token_loss = jnp.log(totals[0, 0, 0, 0]) - jnp.sum(logits[0, 0, 0] * classes[0, 0, 0], axis=0)

    d_parts = jnp.concatenate(
        split_bf(d_logits.reshape(depth, 2 * n, label_count, tok_count), 2)
        + [weight_parts[:, :, : 16 - 2 * label_count]],
        axis=2,
    )

    keys = jnp.concatenate([all_features[1 : 1 + label_count]] * 2)
    keys = jnp.concatenate([keys, jnp.zeros((16 - 2 * label_count, model_width), F32)]).astype(BF)

    def gradient_rows(out_ref, keys_ref, pos_ref, parts_ref):
        chosen = wide_selector(pos_ref, 2 * n, cap)
        parts = jnp.concatenate([parts_ref[0, b] for b in range(2 * n)], axis=1)
        picked = lax.dot_general(chosen, parts, (((1,), (1,)), ((), ())), preferred_element_type=F32)
        first = 2 * label_count
        weight = picked[:, first : first + 1] + picked[:, first + 1 : first + 2] + picked[:, first + 2 : first + 3]
        head_term = jnp.dot(picked.astype(BF), keys_ref[...], preferred_element_type=F32)
        for b in range(2 * n):
            part = slice(b * cap, (b + 1) * cap)
            value = head_term[part] + out_ref[0, b].astype(F32)
            out_ref[0, b] = (value.astype(BF).astype(F32) * weight[part]).astype(BF)

    grads_in = assemble(
        place,
        later,
        one,
        gradient_rows,
        [keys, pos_own, d_parts],
        [
            whole_spec(keys.shape),
            pl.BlockSpec((1, 2 * n, 1, tok_count), lambda z, *_: (z, 0, 0, 0)),
            pl.BlockSpec((1, 2 * n, 16, tok_count), lambda z, *_: (z, 0, 0, 0)),
        ],
        [crossed],
        model_width,
        "gradient_rows",
    ).reshape(row_count, model_width)

    d_active = against(grads_in, down_weight)
    d_gate = (d_active * up_pre * sigma * (1.0 + gate_pre * (1.0 - sigma))).astype(BF)
    d_up = (d_active * gate_pre * sigma).astype(BF)

    d_rows = column_product(
        place, [(d_gate, gate_weight), (d_up, up_weight)], None, list(out_dense[:1]), two, depth, n, cap, width, "d_rows"
    )
    mixed = z_reduce(out_column, n)
    d_column = [None] * depth
    after = []
    for rows, members in reversed(list(zip(d_rows, two))):
        sums = first_sum(spread_back(rows, send_core(rows[1]), after, pos, members[0], n, cap))
        after = [mixed, sums]
        for i, k in enumerate(members):
            d_column[k] = sums[i]
    d_normed = z_reduce(d_column, n)

    grad_down = over_rows(active, grads_in)
    grad_gate = over_rows(d_gate, received)
    grad_up = over_rows(d_up, received)

    outcome = (hidden_wide + mixed).astype(BF)
    d_outcome = lax.dot_general(
        d_logits[0, 0, 0], own_head, (((0,), (0,)), ((), ())), precision=EXACT
    ) + grad_later.astype(F32)
    d_scaled = d_normed * own_gain[None, :]
    products = jnp.sum(d_scaled * hidden_wide, axis=1)
    slope = products
    for j in range(1, n):
        slope = slope + send_y(products, j)
    slope = slope[:, None] / model_width
    d_hidden = inv_rms * d_scaled - hidden_wide * (inv_rms * inv_rms * inv_rms) * slope
    grad_input = (d_outcome + d_hidden).astype(BF)
    return token_loss, outcome, grad_input, grad_gate, grad_up, grad_down


def solution(mesh):
    in_specs = (
        P("ep", "tp"),
        P("tp"),
        P("ep", None),
        P("ep", None),
        P("ep"),
        P("ep", "tp"),
        P("tp", None),
        P(("ep", "tp"), None),
        P(("ep", "tp"), None),
        P(("ep", "tp"), None),
    )
    out_specs = (
        P("ep"),
        P("ep", "tp"),
        P("ep", "tp"),
        P(("ep", "tp"), None),
        P(("ep", "tp"), None),
        P(("ep", "tp"), None),
    )
    return jax.shard_map(shards, mesh=mesh, in_specs=in_specs, out_specs=out_specs, check_vma=False)
```
